256 devices in a mesh: seq: 8 (over z_lo, x), dp: 32 (over z_hi, y, core).
Axes of the slice: x: 4, y: 4, z: 8 (z_hi: 4, z_lo: 2; z = z_hi * 2 + z_lo), core: 2. Of those that a mesh axis runs over, the one named last changes fastest.
Arguments:
- queries: bfloat16 [32, 1024, 2048], P('dp', None, 'seq'), may hold values from -8 to 8
- key_heads: bfloat16 [32, 1024, 1024], P('dp', None, 'seq'), may hold values from -8 to 8
- value_heads: bfloat16 [32, 1024, 1024], P('dp', None, 'seq'), may hold values from -6 to 6
- grad_out: bfloat16 [32, 1024, 2048], P('dp', 'seq'), may hold values from -6 to 6
- features: bfloat16 [32, 1024, 4096], P('dp', 'seq'), may hold values from -6 to 6
Outputs:
- query_grad: bfloat16 [32, 1024, 2048], P('dp', 'seq')
- key_grad: bfloat16 [32, 1024, 1024], P('dp', 'seq')
- weight_grad: float32 [4096, 1024], P('dp', 'seq')
The draws below stay inside these ranges and needn't reach their ends.
All inputs are finite; a program needn't handle non-finite values.
Results may differ from the reference program's by a relative error of at most 0.0058.
Values may be sent and summed in bfloat16 or wider, within the bound.
No kernel may reach another device: no remote copies, remote signals or barrier semaphores. Data moves between devices by JAX's collectives and lax.ppermute only.
A program may use at most 128 MiB of HBM per device.

```python
import math
import jax
import jax.numpy as jnp
from jax import lax

D = 4096
HEADS = 16
KV = 8
HD = 128
LEN = 1024
SEQS = 32


def draw_queries(key, part):
    key = jax.random.fold_in(key, 3)
    base = jax.random.normal(jax.random.fold_in(key, 1), (SEQS, LEN, HEADS * HD), jnp.float32)
    base = jnp.clip(base, -6.0, 6.0)
    return base.astype(jnp.bfloat16)


def draw_key_heads(key, part):
    key = jax.random.fold_in(key, 5)
    base = jax.random.normal(jax.random.fold_in(key, 1), (SEQS, LEN, KV * HD), jnp.float32)
    base = jnp.clip(base, -6.0, 6.0)
    return base.astype(jnp.bfloat16)


def spiked(values, own_key, source, target, blocks, factor):
    def block_of(axis_at):
        return (jnp.arange(values.shape[axis_at]) // (values.shape[axis_at] // blocks)).reshape((-1,) + (1,) * (values.ndim - 1 - axis_at))

    one_side = jax.random.permutation(own_key, blocks)[block_of(target)]
    other_side = (block_of(target) + blocks // 2) % blocks
    return jnp.where((block_of(source) == one_side) | (block_of(source) == other_side), factor * values, values)


def level_of(own_key, extent, cuts, low, high):
    loudness = 1.0
    for dim, blocks in cuts:
        steps = jax.random.uniform(jax.random.fold_in(jax.random.fold_in(own_key, 6), dim), (blocks,), jnp.float32, low / len(cuts), high / len(cuts))
        loudness = loudness * jnp.repeat(jnp.exp(steps), extent[dim] // blocks).reshape((-1,) + (1,) * (len(extent) - 1 - dim))
    return loudness


def gaussian(key, extent, deviation, most, split=(), kind=jnp.bfloat16):
    drawn = deviation * jax.random.normal(key, extent, jnp.float32)
    if split:
        drawn = drawn * level_of(key, extent, split, -0.22, 0.18)
    return jnp.clip(drawn, -most, most).astype(kind)


def noise_with(key, extent, scale, limit, cuts, heavy, kind=jnp.bfloat16):
    entries = scale * jax.random.normal(key, extent, jnp.float32)
    if cuts:
        entries = entries * level_of(key, extent, cuts, -0.22, 0.18)
    return jnp.clip(spiked(entries, jax.random.fold_in(key, 3), *heavy), -limit, limit).astype(kind)


def setup_inputs(seed: int = 0) -> dict:
    arg_keys = jax.random.split(jax.random.key(seed), 6)
    queries = draw_queries(jax.random.fold_in(arg_keys[5], 71), 0)
    key_heads = draw_key_heads(jax.random.fold_in(arg_keys[5], 71), 0)
    value_heads = gaussian(arg_keys[2], (SEQS, LEN, KV * HD), 1.0, 6.0, ((0, 32), (2, 8)))
    grad_out = gaussian(arg_keys[3], (SEQS, LEN, HEADS * HD), 1.0, 6.0, ((0, 32), (1, 8)))
    features = noise_with(arg_keys[4], (SEQS, LEN, D), 1.0, 6.0, ((0, 32), (1, 8)), (0, 2, 32, 2.75))
    return {"queries": queries, "key_heads": key_heads, "value_heads": value_heads, "grad_out": grad_out, "features": features}


def group_grads(query_group, key_rows, value_rows, cot_group):
    group_size = query_group.shape[0]
    length = query_group.shape[1]
    head_size = query_group.shape[2]
    inv_root = 1.0 / math.sqrt(head_size)
    nblocks = max(1, length // 512)
    block_rows = length // nblocks
    key_acc = jnp.zeros((length, head_size), jnp.float32)
    value_acc = jnp.zeros((length, head_size), jnp.float32)
    query_out = []
    contract_rows = (((0,), (0,)), ((), ()))
    contract_cols = (((1,), (1,)), ((), ()))
    for head_idx in range(group_size):
        pieces = []
        for block_idx in range(nblocks):
            row_start = block_idx * block_rows
            row_stop = row_start + block_rows
            query_block = query_group[head_idx, row_start:row_stop]
            cot_block = cot_group[head_idx, row_start:row_stop]
            key_part = key_rows[:row_stop]
            value_part = value_rows[:row_stop]
            scores = lax.dot_general(query_block, key_part, contract_cols, preferred_element_type=jnp.float32) * inv_root
            row_pos = lax.broadcasted_iota(jnp.int32, scores.shape, 0) + row_start
            col_pos = lax.broadcasted_iota(jnp.int32, scores.shape, 1)
            scores = jnp.where(col_pos <= row_pos, scores, -jnp.inf)
            row_max = lax.optimization_barrier(jnp.max(scores, axis=1, keepdims=True))
            weights = jnp.exp(scores - row_max)
            probs = weights / lax.optimization_barrier(jnp.sum(weights, axis=1, keepdims=True))
            probs_b = probs.astype(jnp.bfloat16)
            value_acc = value_acc.at[:row_stop].add(lax.dot_general(probs_b, cot_block, contract_rows, preferred_element_type=jnp.float32))
            dprobs = lax.dot_general(cot_block, value_part, contract_cols, preferred_element_type=jnp.float32)
            row_dot = lax.optimization_barrier(jnp.sum(probs * dprobs, axis=1, keepdims=True))
            score_grad = (probs * (dprobs - row_dot)).astype(jnp.bfloat16)
            pieces.append((jnp.dot(score_grad, key_part, preferred_element_type=jnp.float32) * inv_root).astype(jnp.bfloat16))
            key_acc = key_acc.at[:row_stop].add(lax.dot_general(score_grad, query_block, contract_rows, preferred_element_type=jnp.float32))
        query_out.append(jnp.concatenate(pieces, axis=0))
    return (jnp.stack(query_out), (key_acc * inv_root).astype(jnp.bfloat16), value_acc.astype(jnp.bfloat16))

def reference(queries, key_heads, value_heads, grad_out, features):
    group_size = HEADS // KV

    def one_sequence(items):
        query_seq, key_seq, value_seq, cot_seq = items
        query_split = query_seq.reshape(LEN, KV, group_size, HD).transpose(1, 2, 0, 3)
        cot_split = cot_seq.reshape(LEN, KV, group_size, HD).transpose(1, 2, 0, 3)
        key_split = key_seq.reshape(LEN, KV, HD).transpose(1, 0, 2)
        value_split = value_seq.reshape(LEN, KV, HD).transpose(1, 0, 2)
        query_part, key_part, value_part = lax.map(lambda parts: group_grads(*parts), (query_split, key_split, value_split, cot_split))
        query_tok = query_part.transpose(2, 0, 1, 3).reshape(LEN, HEADS * HD)
        key_tok = key_part.transpose(1, 0, 2).reshape(LEN, KV * HD)
        value_tok = value_part.transpose(1, 0, 2).reshape(LEN, KV * HD)
        return (query_tok, key_tok, value_tok)
    query_grad, key_grad, value_grad = lax.map(one_sequence, (queries, key_heads, value_heads, grad_out))
    weight_grad = lax.dot_general(features.reshape(SEQS * LEN, D), value_grad.reshape(SEQS * LEN, KV * HD), (((0,), (0,)), ((), ())), preferred_element_type=jnp.float32)
    return (query_grad, key_grad, weight_grad)
```

```python
import functools
import math

import jax
import jax.numpy as jnp
from jax import lax
from jax.experimental import pallas as pl
from jax.experimental.pallas import tpu as pltpu
from jax.sharding import Mesh
from jax.sharding import PartitionSpec as P

HD = 128
BLK = 256
NN = (((1,), (0,)), ((), ()))
NT = (((1,), (1,)), ((), ()))
F32 = jnp.float32
BF16 = jnp.bfloat16
VMEM_LIMIT = 48 * 1024 * 1024


def dot(a, b, dims):
    return lax.dot_general(a, b, dims, preferred_element_type=F32)


def probs_kernel(q_ref, k_ref, p_ref):
    length = k_ref.shape[0]
    inv_root = 1.0 / math.sqrt(HD)
    for start in range(0, length, BLK):
        stop = start + BLK
        scores = dot(k_ref[:stop], q_ref[start:stop], NT) * inv_root
        shape = (BLK, BLK)
        keep = lax.broadcasted_iota(jnp.int32, shape, 0) <= lax.broadcasted_iota(
            jnp.int32, shape, 1
        )
        last = jnp.where(keep, scores[start:], -jnp.inf)
        if start:
            scores = jnp.concatenate([scores[:start], last], axis=0)
        else:
            scores = last
        weights = jnp.exp(scores - jnp.max(scores, axis=0, keepdims=True))
        scale = 1.0 / jnp.sum(weights, axis=0, keepdims=True)
        p_ref[0, :stop, start:stop] = (weights * scale).astype(BF16)


def value_kernel(p_ref, cot_ref, out_ref):
    length = cot_ref.shape[0]
    for jstart in range(0, length, BLK):
        jstop = jstart + BLK
        total = jnp.zeros((BLK, HD), F32)
        for head in range(2):
            total += dot(
                p_ref[head, jstart:jstop, jstart:],
                cot_ref[jstart:, head * HD : (head + 1) * HD],
                NN,
            )
        out_ref[:, jstart:jstop] = total.T.astype(BF16)


def grads_kernel(p_ref, q_ref, k_ref, v_ref, cot_ref, out_ref, kt_ref, dk_ref):
    length = k_ref.shape[0]
    inv_root = 1.0 / math.sqrt(HD)
    kt_ref[...] = k_ref[...].T
    dk_ref[...] = jnp.zeros_like(dk_ref)
    for head in range(2):
        cols = slice(head * HD, (head + 1) * HD)
        for start in range(0, length, BLK):
            stop = start + BLK
            dprobs = dot(v_ref[:stop], cot_ref[start:stop, cols], NT)
            probs = p_ref[head, :stop, start:stop].astype(F32)
            row_dot = jnp.sum(probs * dprobs, axis=0, keepdims=True) / jnp.sum(
                probs, axis=0, keepdims=True
            )
            score_grad = (probs * (dprobs - row_dot)).astype(BF16)
            dk_ref[:stop] += dot(score_grad, q_ref[start:stop, cols], NN)
            dq_t = dot(kt_ref[:, :stop], score_grad, NN) * inv_root
            out_ref[start:stop, cols] = dq_t.T.astype(BF16)
    out_ref[:, 2 * HD :] = (dk_ref[...] * inv_root).astype(BF16)


def params():
    return pltpu.CompilerParams(vmem_limit_bytes=VMEM_LIMIT)


def probs_of(q, k):
    length = k.shape[0]
    return pl.pallas_call(
        probs_kernel,
        grid=(2,),
        in_specs=[
            pl.BlockSpec((length, HD), lambda h: (0, h)),
            pl.BlockSpec((length, HD), lambda h: (0, 0)),
        ],
        out_specs=pl.BlockSpec((1, length, length), lambda h: (h, 0, 0)),
        out_shape=jax.ShapeDtypeStruct((2, length, length), BF16),
        compiler_params=params(),
        cost_estimate=pl.CostEstimate(
            flops=4 * length * length * HD, bytes_accessed=5 << 20, transcendentals=length * length
        ),
    )(q, k)


def value_grad_of(probs, cot):
    length = cot.shape[0]
    return pl.pallas_call(
        value_kernel,
        out_shape=jax.ShapeDtypeStruct((HD, length), BF16),
        compiler_params=params(),
        cost_estimate=pl.CostEstimate(
            flops=4 * length * length * HD, bytes_accessed=5 << 20, transcendentals=0
        ),
    )(probs, cot)


def grads_of(probs, q, k, v, cot):
    length = cot.shape[0]
    return pl.pallas_call(
        grads_kernel,
        out_shape=jax.ShapeDtypeStruct((length, 3 * HD), BF16),
        scratch_shapes=[pltpu.VMEM((HD, length), BF16), pltpu.VMEM((length, HD), F32)],
        compiler_params=params(),
        cost_estimate=pl.CostEstimate(
            flops=16 * length * length * HD, bytes_accessed=6 << 20, transcendentals=0
        ),
    )(probs, q, k, v, cot)


def shift(array, axis, size, by):
    return lax.ppermute(array, axis, [(i, (i + by) % size) for i in range(size)])


def on_device(queries, key_heads, value_heads, grad_out, features):
    q, k, v = queries[0], key_heads[0], value_heads[0]
    length = q.shape[0]
    seq = ("z_lo", "x")
    x, z_lo, z_hi = lax.axis_index("x"), lax.axis_index("z_lo"), lax.axis_index("z_hi")
    core = lax.axis_index("core")
    tok = grad_out.shape[1]

    cot_parts = grad_out[0].reshape(tok, 8, 2 * HD).transpose(1, 0, 2)
    cot = lax.all_to_all(cot_parts, seq, 0, 0).reshape(length, 2 * HD)

    width = features.shape[2] // 4
    feat_parts = features[0].reshape(tok, 4, width).transpose(1, 0, 2)
    feat_own = lax.all_to_all(feat_parts, "x", 0, 0).reshape(4 * tok, width)
    feat_other = shift(feat_own, "z_lo", 2, 1)

    probs = probs_of(q, k)
    dv = value_grad_of(probs, cot)

    left = shift(dv, "x", 4, 1)
    right = shift(dv, "x", 4, -1)
    half = length // 2
    far_a = shift(left[:, :half], "x", 4, 1)
    far_b = shift(right[:, half:], "x", 4, -1)

    moved = grads_of(probs, q, k, v, cot)
    moved = lax.all_to_all(moved.reshape(8, tok, 3 * HD), seq, 0, 0)
    query_grad = moved[:, :, : 2 * HD].transpose(1, 0, 2).reshape(1, tok, 16 * HD)
    key_grad = moved[:, :, 2 * HD :].transpose(1, 0, 2).reshape(1, tok, 8 * HD)

    far = jnp.concatenate([far_a, far_b], axis=1)
    values = jnp.concatenate([dv, right, far, left], axis=0)
    own = lax.dynamic_slice_in_dim(values, z_lo * half, half, 1)
    other = lax.dynamic_slice_in_dim(values, (1 - z_lo) * half, half, 1)
    partial = dot(own, feat_own, NN) + dot(other, feat_other, NN)
    partial = partial.reshape(4 * HD, 4, 2, HD)
    keep = lax.dynamic_index_in_dim(partial, core, 2, keepdims=False)
    send = lax.dynamic_index_in_dim(partial, 1 - core, 2, keepdims=False).astype(BF16)
    keep = keep + shift(send.transpose(1, 0, 2), "core", 2, 1).astype(F32).transpose(1, 0, 2)
    keep = keep.transpose(1, 0, 2).astype(BF16)
    over_y = lax.all_to_all(keep, "y", 0, 0)
    summed = jnp.sum(over_y.astype(F32), axis=0).astype(BF16).reshape(4, HD, HD)
    total = jnp.zeros((HD, HD), F32)
    for step in range(4):
        block = lax.dynamic_index_in_dim(summed, (z_hi + step - x) % 4, 0, keepdims=False)
        pairs = [
            (sx * 4 + sz, ((sz + step) % 4) * 4 + sx) for sx in range(4) for sz in range(4)
        ]
        total += lax.ppermute(block, ("x", "z_hi"), pairs).astype(F32)
    return query_grad, key_grad, total.T


def solution(mesh):
    fine = Mesh(mesh.devices.reshape(2, 4, 4, 4, 2), ("z_lo", "x", "z_hi", "y", "core"))
    seq, dp = ("z_lo", "x"), ("z_hi", "y", "core")
    return jax.shard_map(
        on_device,
        mesh=fine,
        in_specs=(P(dp, None, seq), P(dp, None, seq), P(dp, None, seq), P(dp, seq, None), P(dp, seq, None)),
        out_specs=(P(dp, seq, None), P(dp, seq, None), P(dp, seq)),
        check_vma=False,
    )
```

```python
import math

import jax
import jax.numpy as jnp
from jax import lax
from jax.experimental import pallas as pl
from jax.experimental.pallas import tpu as pltpu
from jax.sharding import Mesh
from jax.sharding import PartitionSpec as P

HD = 128
BLK = 256
NN = (((1,), (0,)), ((), ()))
NT = (((1,), (1,)), ((), ()))
F32 = jnp.float32
BF16 = jnp.bfloat16
VMEM_LIMIT = 24 * 1024 * 1024
LONG = 1 << 35


def dot(a, b, dims):
    return lax.dot_general(a, b, dims, preferred_element_type=F32)


def probs_kernel(q_ref, k_ref, p_ref, buf_ref, sems):
    length = k_ref.shape[0]
    inv_root = 1.0 / math.sqrt(HD)
    shape = (BLK, BLK)
    keep = lax.broadcasted_iota(jnp.int32, shape, 0) <= lax.broadcasted_iota(jnp.int32, shape, 1)
    copies = []
    for head in range(2):
        for start in range(0, length, BLK):
            stop = start + BLK
            q_block = q_ref[start:stop, head * HD : (head + 1) * HD]
            scores = dot(k_ref[:stop], q_block, NT) * inv_root
            last = jnp.where(keep, scores[start:], -jnp.inf)
            if start:
                scores = jnp.concatenate([scores[:start], last], axis=0)
            else:
                scores = last
            weights = jnp.exp(scores - jnp.max(scores, axis=0, keepdims=True))
            scale = 1.0 / jnp.sum(weights, axis=0, keepdims=True)
            buf_ref[head, :stop, start:stop] = (weights * scale).astype(BF16)
            part = (head, pl.ds(0, stop), pl.ds(start, BLK))
            copies.append(
                pltpu.make_async_copy(buf_ref.at[part], p_ref.at[part], sems.at[len(copies)])
            )
            copies[-1].start()
    for copy in copies:
        copy.wait()


def value_kernel(p_ref, cot_ref, out_ref):
    length = cot_ref.shape[0]
    for jstart in range(0, length, BLK):
        jstop = jstart + BLK
        total = jnp.zeros((BLK, HD), F32)
        for head in range(2):
            total += dot(
                p_ref[head, jstart:jstop, jstart:],
                cot_ref[jstart:, head * HD : (head + 1) * HD],
                NN,
            )
        out_ref[:, jstart:jstop] = total.T.astype(BF16)


def grads_kernel(p_ref, q_ref, k_ref, v_ref, cot_ref, out_ref, kt_ref, dk_ref):
    length = k_ref.shape[0]
    inv_root = 1.0 / math.sqrt(HD)
    kt_ref[...] = k_ref[...].T
    dk_ref[...] = jnp.zeros_like(dk_ref)

    for head in range(2):
        cols = slice(head * HD, (head + 1) * HD)
        for start in range(0, length, BLK):
            stop = start + BLK
            dprobs = dot(v_ref[:stop], cot_ref[start:stop, cols], NT)
            probs = p_ref[head, :stop, start:stop].astype(F32)
            row_dot = jnp.sum(probs * dprobs, axis=0, keepdims=True) / jnp.sum(
                probs, axis=0, keepdims=True
            )
            score_grad = (probs * (dprobs - row_dot)).astype(BF16)
            dk_ref[:stop] += dot(score_grad, q_ref[start:stop, cols], NN)
            dq_t = dot(kt_ref[:, :stop], score_grad, NN) * inv_root
            out_ref[start:stop, cols] = dq_t.T.astype(BF16)
    out_ref[:, 2 * HD :] = (dk_ref[...] * inv_root).astype(BF16)


def params():
    return pltpu.CompilerParams(vmem_limit_bytes=VMEM_LIMIT)


def in_hbm(array):
    return pltpu.with_memory_space_constraint(array, pltpu.HBM)


def probs_of(q, k):
    length = k.shape[0]
    vmem = pl.BlockSpec(memory_space=pltpu.VMEM)
    return pl.pallas_call(
        probs_kernel,
        in_specs=[vmem, vmem],
        out_specs=pl.BlockSpec(memory_space=pl.ANY),
        out_shape=pltpu.HBM((2, length, length), BF16),
        scratch_shapes=[pltpu.VMEM((2, length, length), BF16), pltpu.SemaphoreType.DMA((8,))],
        compiler_params=params(),
        cost_estimate=pl.CostEstimate(
            flops=LONG, bytes_accessed=5 << 20, transcendentals=length * length
        ),
    )(in_hbm(q), in_hbm(k))


def grads_of(place, probs, q, k, v, cot, after):
    length = cot.shape[0]
    return call(
        grads_kernel,
        shape_of(length, 3 * HD),
        probs, q, k, v, cot,
        after=[after],
        flops=LONG,
        nbytes=6 << 20,
        scratch=[pltpu.VMEM((HD, length), BF16), pltpu.VMEM((length, HD), F32)],
    )


def pack_cot_kernel(cot_ref, out_ref):
    for dest in range(8):
        out_ref[dest] = cot_ref[:, dest * 2 * HD : (dest + 1) * 2 * HD]


def pack_features_kernel(place_ref, f_ref, *out_refs):
    width = out_refs[0].shape[1]
    for step, ref in enumerate(out_refs):
        start = pl.multiple_of(lax.rem(place_ref[0] + step, 4) * width, width)
        ref[...] = f_ref[:, pl.ds(start, width)]


def gate_kernel():
    pass


def product_kernel(place_ref, *refs):
    v_refs, f_refs, (keep_ref, send_ref, v_ref, f_ref, sems) = refs[:4], refs[4:12], refs[12:]
    x, core, z_lo = place_ref[0], place_ref[1], place_ref[2]
    tok = f_refs[0].shape[0]
    copies = []
    for step, ref in enumerate(v_refs):
        rows = pl.ds(pl.multiple_of(lax.rem(x + step, 4) * HD, HD), HD)
        copies.append(pltpu.make_async_copy(ref, v_ref.at[rows], sems.at[step]))
    for index, ref in enumerate(f_refs):
        block = lax.rem(z_lo + index // 4, 2) * 4 + lax.rem(x + 4 - index % 4, 4)
        rows = pl.ds(pl.multiple_of(block * tok, tok), tok)
        copies.append(pltpu.make_async_copy(ref, f_ref.at[rows], sems.at[4 + index]))
    for copy in copies:
        copy.start()
    for copy in copies:
        copy.wait()
    for y in range(4):
        total = dot(v_ref[...], f_ref[:, y * 2 * HD : (y + 1) * 2 * HD], NN)
        mine = jnp.where(core == 0, total[:, :HD], total[:, HD:])
        other = jnp.where(core == 0, total[:, HD:], total[:, :HD]).astype(BF16)
        for e in range(4):
            keep_ref[e, y] = mine[e * HD : (e + 1) * HD]
            send_ref[e, y] = other[e * HD : (e + 1) * HD]


def add_kernel(keep_ref, got_ref, out_ref):
    out_ref[...] = (keep_ref[...] + got_ref[...].astype(F32)).astype(BF16)


def sum_kernel(got_ref, out_ref):
    for x in range(4):
        total = got_ref[x, 0].astype(F32)
        for y in range(1, 4):
            total += got_ref[x, y].astype(F32)
        out_ref[x] = total.astype(BF16)


def last_kernel(got_ref, out_ref):
    total = got_ref[0].astype(F32)
    for z in range(1, 4):
        total += got_ref[z].astype(F32)
    out_ref[...] = total.T


def assemble_kernel(got_ref, q_ref, k_ref):
    for src in range(8):
        q_ref[:, src * 2 * HD : (src + 1) * 2 * HD] = got_ref[src, :, : 2 * HD]
        k_ref[:, src * HD : (src + 1) * HD] = got_ref[src, :, 2 * HD :]


def call(
    kernel, shapes, *args, place=None, after=(), behind=(), anywhere=False, flops=0,
    nbytes=1 << 20, scratch=(),
):
    space = pltpu.MemorySpace.HBM if anywhere else pltpu.VMEM
    specs = [pl.BlockSpec(memory_space=space)] * len(args)
    shapes = list(shapes) if isinstance(shapes, (list, tuple)) else [shapes]
    out_specs = [pl.BlockSpec(memory_space=pltpu.VMEM)] * len(shapes)
    if place is not None:
        args = (place,) + args
        specs = [pl.BlockSpec(memory_space=pltpu.SMEM)] + specs
    n_in, n_out, n_after, n_behind = len(args), len(shapes), len(after), len(behind)
    args += tuple(after) + tuple(behind)
    specs += [pl.BlockSpec(memory_space=pl.ANY)] * (n_after + n_behind)
    shapes += [jax.ShapeDtypeStruct(x.shape, x.dtype) for x in behind]
    out_specs += [pl.BlockSpec(memory_space=pl.ANY)] * n_behind
    first_out = n_in + n_after + n_behind

    def body(*refs):
        outs = refs[first_out : first_out + n_out]
        kernel(*refs[:n_in], *outs, *refs[first_out + n_out + n_behind :])

    outs = pl.pallas_call(
        body,
        out_shape=shapes,
        in_specs=specs,
        out_specs=out_specs,
        scratch_shapes=list(scratch),
        input_output_aliases={n_in + n_after + i: n_out + i for i in range(n_behind)},
        compiler_params=params(),
        cost_estimate=pl.CostEstimate(flops=flops, bytes_accessed=nbytes, transcendentals=0),
    )(*args)
    return outs if len(outs) > 1 else outs[0]


def shape_of(*dims, dtype=BF16):
    return jax.ShapeDtypeStruct(dims, dtype)


def shift(array, axis, size, by):
    return lax.ppermute(array, axis, [(i, (i + by) % size) for i in range(size)])


def on_device(queries, key_heads, value_heads, grad_out, features):
    q, k, v = queries[0], key_heads[0], value_heads[0]
    length = q.shape[0]
    seq = ("z_lo", "x")
    place = jnp.stack([lax.axis_index(a) for a in ("x", "core", "z_lo")]).astype(jnp.int32)
    tok = grad_out.shape[1]
    width = features.shape[2] // 4

    cot_parts = call(pack_cot_kernel, shape_of(8, tok, 2 * HD), grad_out[0])
    cot = lax.all_to_all(cot_parts, seq, 0, 0).reshape(length, 2 * HD)

    parts = call(
        pack_features_kernel, [shape_of(tok, width)] * 4, features[0], place=place, nbytes=2 << 20
    )
    near = [shift(parts[step], "x", 4, step) for step in range(1, 4)]
    far = shift(parts[0], "z_lo", 2, 1)

    probs = probs_of(q, k)
    dv = call(value_kernel, shape_of(HD, length), probs, cot, flops=1 << 29, nbytes=5 << 20)
    near = [call(gate_kernel, [], after=[dv], behind=[part]) for part in near]
    feats = [parts[0], *near, far] + [shift(part, "z_lo", 2, 1) for part in near]

    values = [dv] + [shift(dv, "x", 4, -step) for step in range(1, 4)]

    moved = grads_of(place, probs, q, k, v, cot, dv)
    keep, send = call(
        product_kernel,
        (shape_of(4, 4, HD, HD, dtype=F32), shape_of(4, 4, HD, HD)),
        *[in_hbm(block) for block in values + feats],
        place=place,
        after=[moved],
        anywhere=True,
        flops=LONG,
        nbytes=5 << 20,
        scratch=[
            pltpu.VMEM((4 * HD, length), BF16),
            pltpu.VMEM((length, width), BF16),
            pltpu.SemaphoreType.DMA((12,)),
        ],
    )
    got = lax.all_to_all(moved.reshape(8, tok, 3 * HD), seq, 0, 0)
    send = call(gate_kernel, [], after=[got], behind=[send])
    both = call(add_kernel, shape_of(4, 4, HD, HD), keep, shift(send, "core", 2, 1))
    over_y = lax.all_to_all(both.reshape(16, HD, HD), ("x", "y"), 0, 0).reshape(4, 4, HD, HD)
    summed = call(sum_kernel, shape_of(4, HD, HD), over_y, flops=LONG)
    over_z = lax.all_to_all(summed, "z_hi", 0, 0)
    query_grad, key_grad = call(
        assemble_kernel,
        (shape_of(tok, 16 * HD), shape_of(tok, 8 * HD)),
        got,
        after=[both],
    )
    weight_grad = call(last_kernel, shape_of(HD, HD, dtype=F32), over_z)
    return query_grad[None], key_grad[None], weight_grad


def solution(mesh):
    fine = Mesh(mesh.devices.reshape(2, 4, 4, 4, 2), ("z_lo", "x", "z_hi", "y", "core"))
    seq, dp = ("z_lo", "x"), ("z_hi", "y", "core")
    return jax.shard_map(
        on_device,
        mesh=fine,
        in_specs=(P(dp, None, seq), P(dp, None, seq), P(dp, None, seq), P(dp, seq, None), P(dp, seq, None)),
        out_specs=(P(dp, seq, None), P(dp, seq, None), P(dp, seq)),
        check_vma=False,
    )
```

```python
import math

import jax
import jax.numpy as jnp
from jax import lax
from jax.experimental import pallas as pl
from jax.experimental.pallas import tpu as pltpu
from jax.sharding import Mesh
from jax.sharding import PartitionSpec as P

HD = 128
BLK = 256
NN = (((1,), (0,)), ((), ()))
NT = (((1,), (1,)), ((), ()))
F32 = jnp.float32
BF16 = jnp.bfloat16
VMEM_LIMIT = 24 * 1024 * 1024
LONG = 1 << 35


def dot(a, b, dims):
    return lax.dot_general(a, b, dims, preferred_element_type=F32)


def probs_kernel(q_ref, k_ref, p_ref, buf_ref, sems):
    length = k_ref.shape[0]
    inv_root = 1.0 / math.sqrt(HD)
    shape = (BLK, BLK)
    keep = lax.broadcasted_iota(jnp.int32, shape, 0) <= lax.broadcasted_iota(jnp.int32, shape, 1)
    copies = []
    for head in range(2):
        for start in range(0, length, BLK):
            stop = start + BLK
            q_block = q_ref[start:stop, head * HD : (head + 1) * HD]
            scores = dot(k_ref[:stop], q_block, NT) * inv_root
            last = jnp.where(keep, scores[start:], -jnp.inf)
            if start:
                scores = jnp.concatenate([scores[:start], last], axis=0)
            else:
                scores = last
            weights = jnp.exp(scores - jnp.max(scores, axis=0, keepdims=True))
            scale = 1.0 / jnp.sum(weights, axis=0, keepdims=True)
            buf_ref[head, :stop, start:stop] = (weights * scale).astype(BF16)
            part = (head, pl.ds(0, stop), pl.ds(start, BLK))
            copies.append(
                pltpu.make_async_copy(buf_ref.at[part], p_ref.at[part], sems.at[len(copies)])
            )
            copies[-1].start()
    for copy in copies:
        copy.wait()


def value_kernel(p_ref, cot_ref, out_ref):
    length = cot_ref.shape[0]
    for jstart in range(0, length, BLK):
        jstop = jstart + BLK
        total = jnp.zeros((BLK, HD), F32)
        for head in range(2):
            total += dot(
                p_ref[head, jstart:jstop, jstart:],
                cot_ref[jstart:, head * HD : (head + 1) * HD],
                NN,
            )
        out_ref[:, jstart:jstop] = total.T.astype(BF16)


def grads_kernel(place_ref, p_ref, q_ref, k_ref, v_ref, cot_ref, out_ref, kt_ref, dk_ref):
    length = k_ref.shape[0]
    tok = out_ref.shape[2]
    inv_root = 1.0 / math.sqrt(HD)
    kt_ref[...] = k_ref[...].T
    dk_ref[...] = jnp.zeros_like(dk_ref)

    def put(rows, first, cols):
        for part in range(rows.shape[0] // tok):
            block = first // tok + part
            step = lax.rem(block % 4 + 4 - place_ref[0], 4)
            out_ref[step, block // 4, :, cols] = rows[part * tok : (part + 1) * tok]

    for head in range(2):
        cols = slice(head * HD, (head + 1) * HD)
        for start in range(0, length, BLK):
            stop = start + BLK
            dprobs = dot(v_ref[:stop], cot_ref[start:stop, cols], NT)
            probs = p_ref[head, :stop, start:stop].astype(F32)
            row_dot = jnp.sum(probs * dprobs, axis=0, keepdims=True) / jnp.sum(
                probs, axis=0, keepdims=True
            )
            score_grad = (probs * (dprobs - row_dot)).astype(BF16)
            dk_ref[:stop] += dot(score_grad, q_ref[start:stop, cols], NN)
            dq_t = dot(kt_ref[:, :stop], score_grad, NN) * inv_root
            put(dq_t.T.astype(BF16), start, cols)
    put((dk_ref[...] * inv_root).astype(BF16), 0, slice(2 * HD, 3 * HD))


def params():
    return pltpu.CompilerParams(vmem_limit_bytes=VMEM_LIMIT)


def in_hbm(array):
    return pltpu.with_memory_space_constraint(array, pltpu.HBM)


def probs_of(q, k):
    length = k.shape[0]
    vmem = pl.BlockSpec(memory_space=pltpu.VMEM)
    return pl.pallas_call(
        probs_kernel,
        in_specs=[vmem, vmem],
        out_specs=pl.BlockSpec(memory_space=pl.ANY),
        out_shape=pltpu.HBM((2, length, length), BF16),
        scratch_shapes=[pltpu.VMEM((2, length, length), BF16), pltpu.SemaphoreType.DMA((8,))],
        compiler_params=params(),
        cost_estimate=pl.CostEstimate(
            flops=LONG, bytes_accessed=5 << 20, transcendentals=length * length
        ),
    )(in_hbm(q), in_hbm(k))


def grads_of(place, probs, q, k, v, cot, after):
    length = cot.shape[0]
    return call(
        grads_kernel,
        shape_of(4, 2, length // 8, 3 * HD),
        probs, q, k, v, cot,
        place=place,
        after=[after],
        flops=LONG,
        nbytes=6 << 20,
        scratch=[pltpu.VMEM((HD, length), BF16), pltpu.VMEM((length, HD), F32)],
    )


def pack_cot_kernel(cot_ref, out_ref):
    for dest in range(8):
        out_ref[dest] = cot_ref[:, dest * 2 * HD : (dest + 1) * 2 * HD]


def pack_features_kernel(place_ref, f_ref, *out_refs):
    width = out_refs[0].shape[1]
    for step, ref in enumerate(out_refs):
        start = pl.multiple_of(lax.rem(place_ref[0] + step, 4) * width, width)
        ref[...] = f_ref[:, pl.ds(start, width)]


def join_kernel(*refs):
    for index, ref in enumerate(refs[:-1]):
        refs[-1][index] = ref[...]


def gate_kernel():
    pass


def near_kernel(place_ref, *refs):
    v_refs, f_refs, (part_ref, other_ref, v_ref, f_ref) = refs[:4], refs[4:8], refs[8:]
    x, z_lo = place_ref[0], place_ref[2]
    tok, half = f_refs[0].shape[0], other_ref.shape[1]
    for step, ref in enumerate(v_refs):
        rows = pl.ds(pl.multiple_of(lax.rem(x + step, 4) * HD, HD), HD)
        v_ref[rows, :] = ref[:, pl.ds(pl.multiple_of(z_lo * half, half), half)]
        other_ref[rows, :] = ref[:, pl.ds(pl.multiple_of((1 - z_lo) * half, half), half)]
    for step, ref in enumerate(f_refs):
        block = lax.rem(x + 4 - step, 4)
        f_ref[pl.ds(pl.multiple_of(block * tok, tok), tok), :] = ref[...]
    for y in range(4):
        cols = slice(y * 2 * HD, (y + 1) * 2 * HD)
        part_ref[:, cols] = dot(v_ref[...], f_ref[:, cols], NN)


def far_kernel(place_ref, part_ref, v_ref, *refs):
    own_ref, next_ref, rest_ref, keep_ref, send_ref, f_ref = refs
    x, core = place_ref[0], place_ref[1]
    tok = own_ref.shape[0]
    for step, ref in enumerate((own_ref, next_ref, rest_ref.at[0], rest_ref.at[1])):
        block = lax.rem(x + 4 - step, 4)
        f_ref[pl.ds(pl.multiple_of(block * tok, tok), tok), :] = ref[...]
    for y in range(4):
        cols = slice(y * 2 * HD, (y + 1) * 2 * HD)
        total = part_ref[:, cols] + dot(v_ref[...], f_ref[:, cols], NN)
        mine = jnp.where(core == 0, total[:, :HD], total[:, HD:])
        other = jnp.where(core == 0, total[:, HD:], total[:, :HD]).astype(BF16)
        for e in range(4):
            keep_ref[e, y] = mine[e * HD : (e + 1) * HD]
            send_ref[e, y] = other[e * HD : (e + 1) * HD]


def add_kernel(keep_ref, got_ref, out_ref):
    out_ref[...] = (keep_ref[...] + got_ref[...].astype(F32)).astype(BF16)


def sum_kernel(got_ref, out_ref):
    for x in range(4):
        total = got_ref[x, 0].astype(F32)
        for y in range(1, 4):
            total += got_ref[x, y].astype(F32)
        out_ref[x] = total.astype(BF16)


def last_kernel(got_ref, out_ref):
    total = got_ref[0].astype(F32)
    for z in range(1, 4):
        total += got_ref[z].astype(F32)
    out_ref[...] = total.T


def pack_rows_kernel(place_ref, own_ref, a_ref, b_ref, c_ref, out_ref):
    other = 1 - place_ref[2]
    out_ref[0] = own_ref[0, other]
    for step, ref in enumerate((a_ref, b_ref, c_ref)):
        out_ref[step + 1] = ref[other]


def assemble_kernel(place_ref, own_ref, a_ref, b_ref, c_ref, far_ref, q_ref, k_ref):
    x, z_lo = place_ref[0], place_ref[2]

    def put(rows, z, step):
        src = z * 4 + lax.rem(x + 4 - step, 4)
        q_ref[:, pl.ds(pl.multiple_of(src * 2 * HD, 2 * HD), 2 * HD)] = rows[:, : 2 * HD]
        k_ref[:, pl.ds(pl.multiple_of(src * HD, HD), HD)] = rows[:, 2 * HD :]

    put(own_ref[0, z_lo], z_lo, 0)
    for step, ref in enumerate((a_ref, b_ref, c_ref)):
        put(ref[z_lo], z_lo, step + 1)
    for step in range(4):
        put(far_ref[step], 1 - z_lo, step)


def call(
    kernel, shapes, *args, place=None, after=(), behind=(), anywhere=False, flops=0,
    nbytes=1 << 20, scratch=(),
):
    space = pltpu.MemorySpace.HBM if anywhere else pltpu.VMEM
    specs = [pl.BlockSpec(memory_space=space)] * len(args)
    shapes = list(shapes) if isinstance(shapes, (list, tuple)) else [shapes]
    out_specs = [pl.BlockSpec(memory_space=pltpu.VMEM)] * len(shapes)
    if place is not None:
        args = (place,) + args
        specs = [pl.BlockSpec(memory_space=pltpu.SMEM)] + specs
    n_in, n_out, n_after, n_behind = len(args), len(shapes), len(after), len(behind)
    args += tuple(after) + tuple(behind)
    specs += [pl.BlockSpec(memory_space=pl.ANY)] * (n_after + n_behind)
    shapes += [jax.ShapeDtypeStruct(x.shape, x.dtype) for x in behind]
    out_specs += [pl.BlockSpec(memory_space=pl.ANY)] * n_behind
    first_out = n_in + n_after + n_behind

    def body(*refs):
        outs = refs[first_out : first_out + n_out]
        kernel(*refs[:n_in], *outs, *refs[first_out + n_out + n_behind :])

    outs = pl.pallas_call(
        body,
        out_shape=shapes,
        in_specs=specs,
        out_specs=out_specs,
        scratch_shapes=list(scratch),
        input_output_aliases={n_in + n_after + i: n_out + i for i in range(n_behind)},
        compiler_params=params(),
        cost_estimate=pl.CostEstimate(flops=flops, bytes_accessed=nbytes, transcendentals=0),
    )(*args)
    return outs if len(outs) > 1 else outs[0]


def shape_of(*dims, dtype=BF16):
    return jax.ShapeDtypeStruct(dims, dtype)


def shift(array, axis, size, by):
    return lax.ppermute(array, axis, [(i, (i + by) % size) for i in range(size)])


def on_device(queries, key_heads, value_heads, grad_out, features):
    q, k, v = queries[0], key_heads[0], value_heads[0]
    length = q.shape[0]
    seq = ("z_lo", "x")
    place = jnp.stack([lax.axis_index(a) for a in ("x", "core", "z_lo")]).astype(jnp.int32)
    tok = grad_out.shape[1]
    width = features.shape[2] // 4

    cot_parts = call(pack_cot_kernel, shape_of(8, tok, 2 * HD), grad_out[0])
    cot = lax.all_to_all(cot_parts, seq, 0, 0).reshape(length, 2 * HD)

    parts = call(
        pack_features_kernel, [shape_of(tok, width)] * 4, features[0], place=place, nbytes=2 << 20
    )
    near = [shift(parts[step], "x", 4, step) for step in range(1, 4)]
    far = shift(parts[0], "z_lo", 2, 1)

    probs = probs_of(q, k)
    dv = call(
        value_kernel, shape_of(HD, length), probs, cot, after=[far], flops=1 << 29, nbytes=5 << 20
    )
    first = call(gate_kernel, [], after=[dv], behind=near[:1])
    rest = call(join_kernel, shape_of(2, tok, width), *near[1:], after=[dv], nbytes=2 << 20)
    near = [parts[0], first, *near[1:]]
    far = [far, shift(first, "z_lo", 2, 1), shift(rest, "z_lo", 2, 1)]

    values = [dv] + [shift(dv, "x", 4, -step) for step in range(1, 4)]

    moved = grads_of(place, probs, q, k, v, cot, dv)
    half = length // 2
    part, other = call(
        near_kernel,
        [shape_of(4 * HD, width, dtype=F32), shape_of(4 * HD, half)],
        *values, *near,
        place=place,
        after=[moved],
        flops=0,
        nbytes=0,
        scratch=[pltpu.VMEM((4 * HD, half), BF16), pltpu.VMEM((half, width), BF16)],
    )
    keep, send = call(
        far_kernel,
        [shape_of(4, 4, HD, HD, dtype=F32), shape_of(4, 4, HD, HD)],
        part, other, *far,
        place=place,
        flops=LONG,
        nbytes=5 << 20,
        scratch=[pltpu.VMEM((half, width), BF16)],
    )
    got_x = [shift(moved[step], "x", 4, step) for step in range(1, 4)]
    send = call(gate_kernel, [], after=got_x, behind=[send])
    both = call(add_kernel, shape_of(4, 4, HD, HD), keep, shift(send, "core", 2, 1))
    over_y = lax.all_to_all(both.reshape(16, HD, HD), ("x", "y"), 0, 0).reshape(4, 4, HD, HD)
    summed = call(sum_kernel, shape_of(4, HD, HD), over_y, flops=LONG)
    over_z = lax.all_to_all(summed, "z_hi", 0, 0)
    packed = call(
        pack_rows_kernel, shape_of(4, tok, 3 * HD), moved, *got_x, place=place, after=[both]
    )
    got_z = shift(packed, "z_lo", 2, 1)
    query_grad, key_grad = call(
        assemble_kernel,
        (shape_of(tok, 16 * HD), shape_of(tok, 8 * HD)),
        moved, *got_x, got_z,
        place=place,
        after=[summed],
    )
    weight_grad = call(last_kernel, shape_of(HD, HD, dtype=F32), over_z)
    return query_grad[None], key_grad[None], weight_grad


def solution(mesh):
    fine = Mesh(mesh.devices.reshape(2, 4, 4, 4, 2), ("z_lo", "x", "z_hi", "y", "core"))
    seq, dp = ("z_lo", "x"), ("z_hi", "y", "core")
    return jax.shard_map(
        on_device,
        mesh=fine,
        in_specs=(P(dp, None, seq), P(dp, None, seq), P(dp, None, seq), P(dp, seq, None), P(dp, seq, None)),
        out_specs=(P(dp, seq, None), P(dp, seq, None), P(dp, seq)),
        check_vma=False,
    )
```

```python
import math

import jax
import jax.numpy as jnp
from jax import lax
from jax.experimental import pallas as pl
from jax.experimental.pallas import tpu as pltpu
from jax.sharding import Mesh
from jax.sharding import PartitionSpec as P

HD = 128
BLK = 256
NN = (((1,), (0,)), ((), ()))
NT = (((1,), (1,)), ((), ()))
F32 = jnp.float32
BF16 = jnp.bfloat16
VMEM_LIMIT = 24 * 1024 * 1024
LONG = 1 << 35


def dot(a, b, dims):
    return lax.dot_general(a, b, dims, preferred_element_type=F32)


def probs_kernel(q_ref, k_ref, p_ref, buf_ref, sems):
    length = k_ref.shape[0]
    inv_root = 1.0 / math.sqrt(HD)
    shape = (BLK, BLK)
    keep = lax.broadcasted_iota(jnp.int32, shape, 0) <= lax.broadcasted_iota(jnp.int32, shape, 1)
    copies = []
    for head in range(2):
        for start in range(0, length, BLK):
            stop = start + BLK
            q_block = q_ref[start:stop, head * HD : (head + 1) * HD]
            scores = dot(k_ref[:stop], q_block, NT) * inv_root
            last = jnp.where(keep, scores[start:], -jnp.inf)
            if start:
                scores = jnp.concatenate([scores[:start], last], axis=0)
            else:
                scores = last
            weights = jnp.exp(scores - jnp.max(scores, axis=0, keepdims=True))
            scale = 1.0 / jnp.sum(weights, axis=0, keepdims=True)
            buf_ref[head, :stop, start:stop] = (weights * scale).astype(BF16)
            part = (head, pl.ds(0, stop), pl.ds(start, BLK))
            copies.append(
                pltpu.make_async_copy(buf_ref.at[part], p_ref.at[part], sems.at[len(copies)])
            )
            copies[-1].start()
    for copy in copies:
        copy.wait()


def value_kernel(p_ref, cot_ref, out_ref):
    length = cot_ref.shape[0]
    for jstart in range(0, length, BLK):
        jstop = jstart + BLK
        total = jnp.zeros((BLK, HD), F32)
        for head in range(2):
            total += dot(
                p_ref[head, jstart:jstop, jstart:],
                cot_ref[jstart:, head * HD : (head + 1) * HD],
                NN,
            )
        out_ref[:, jstart:jstop] = total.T.astype(BF16)


def grads_kernel(place_ref, p_ref, q_ref, k_ref, v_ref, cot_ref, out_ref, kt_ref, dk_ref):
    length = k_ref.shape[0]
    tok = out_ref.shape[2]
    inv_root = 1.0 / math.sqrt(HD)
    kt_ref[...] = k_ref[...].T
    dk_ref[...] = jnp.zeros_like(dk_ref)

    def put(rows, first, cols):
        for part in range(rows.shape[0] // tok):
            block = first // tok + part
            step = lax.rem(block % 4 + 4 - place_ref[0], 4)
            out_ref[step, block // 4, :, cols] = rows[part * tok : (part + 1) * tok]

    for head in range(2):
        cols = slice(head * HD, (head + 1) * HD)
        for start in range(0, length, BLK):
            stop = start + BLK
            dprobs = dot(v_ref[:stop], cot_ref[start:stop, cols], NT)
            probs = p_ref[head, :stop, start:stop].astype(F32)
            row_dot = jnp.sum(probs * dprobs, axis=0, keepdims=True) / jnp.sum(
                probs, axis=0, keepdims=True
            )
            score_grad = (probs * (dprobs - row_dot)).astype(BF16)
            dk_ref[:stop] += dot(score_grad, q_ref[start:stop, cols], NN)
            dq_t = dot(kt_ref[:, :stop], score_grad, NN) * inv_root
            put(dq_t.T.astype(BF16), start, cols)
    put((dk_ref[...] * inv_root).astype(BF16), 0, slice(2 * HD, 3 * HD))


def params():
    return pltpu.CompilerParams(vmem_limit_bytes=VMEM_LIMIT)


def in_hbm(array):
    return pltpu.with_memory_space_constraint(array, pltpu.HBM)


def probs_of(q, k):
    length = k.shape[0]
    vmem = pl.BlockSpec(memory_space=pltpu.VMEM)
    return pl.pallas_call(
        probs_kernel,
        in_specs=[vmem, vmem],
        out_specs=pl.BlockSpec(memory_space=pl.ANY),
        out_shape=pltpu.HBM((2, length, length), BF16),
        scratch_shapes=[pltpu.VMEM((2, length, length), BF16), pltpu.SemaphoreType.DMA((8,))],
        compiler_params=params(),
        cost_estimate=pl.CostEstimate(
            flops=LONG, bytes_accessed=5 << 20, transcendentals=length * length
        ),
    )(in_hbm(q), in_hbm(k))


def grads_of(place, probs, q, k, v, cot, after):
    length = cot.shape[0]
    return call(
        grads_kernel,
        shape_of(4, 2, length // 8, 3 * HD),
        probs, q, k, v, cot,
        place=place,
        after=[after],
        flops=LONG,
        nbytes=6 << 20,
        scratch=[pltpu.VMEM((HD, length), BF16), pltpu.VMEM((length, HD), F32)],
    )


def pack_cot_kernel(cot_ref, out_ref):
    for dest in range(8):
        out_ref[dest] = cot_ref[:, dest * 2 * HD : (dest + 1) * 2 * HD]


def pack_features_kernel(place_ref, f_ref, *out_refs):
    width = out_refs[0].shape[1]
    for step, ref in enumerate(out_refs):
        start = pl.multiple_of(lax.rem(place_ref[0] + step, 4) * width, width)
        ref[...] = f_ref[:, pl.ds(start, width)]


def join_kernel(*refs):
    for index, ref in enumerate(refs[:-1]):
        refs[-1][index] = ref[...]


def gate_kernel():
    pass


def near_kernel(place_ref, *refs):
    v_refs, f_refs, (part_ref, other_ref, v_ref, f_ref) = refs[:4], refs[4:8], refs[8:]
    x, z_lo = place_ref[0], place_ref[2]
    tok, half = f_refs[0].shape[0], other_ref.shape[1]
    for step, ref in enumerate(v_refs):
        rows = pl.ds(pl.multiple_of(lax.rem(x + step, 4) * HD, HD), HD)
        v_ref[rows, :] = ref[:, pl.ds(pl.multiple_of(z_lo * half, half), half)]
        other_ref[rows, :] = ref[:, pl.ds(pl.multiple_of((1 - z_lo) * half, half), half)]
    for step, ref in enumerate(f_refs):
        block = lax.rem(x + 4 - step, 4)
        f_ref[pl.ds(pl.multiple_of(block * tok, tok), tok), :] = ref[...]
    for y in range(4):
        cols = slice(y * 2 * HD, (y + 1) * 2 * HD)
        part_ref[:, cols] = dot(v_ref[...], f_ref[:, cols], NN)


def far_kernel(place_ref, part_ref, v_ref, *refs):
    own_ref, next_ref, rest_ref, keep_ref, send_ref, f_ref = refs
    x, core = place_ref[0], place_ref[1]
    tok = own_ref.shape[0]
    for step, ref in enumerate((own_ref, next_ref, rest_ref.at[0], rest_ref.at[1])):
        block = lax.rem(x + 4 - step, 4)
        f_ref[pl.ds(pl.multiple_of(block * tok, tok), tok), :] = ref[...]
    for y in range(4):
        cols = slice(y * 2 * HD, (y + 1) * 2 * HD)
        total = part_ref[:, cols] + dot(v_ref[...], f_ref[:, cols], NN)
        mine = jnp.where(core == 0, total[:, :HD], total[:, HD:])
        other = jnp.where(core == 0, total[:, HD:], total[:, :HD]).astype(BF16)
        for e in range(4):
            keep_ref[e, y] = mine[e * HD : (e + 1) * HD]
            send_ref[e, y] = other[e * HD : (e + 1) * HD]


def add_kernel(keep_ref, got_ref, out_ref):
    out_ref[...] = (keep_ref[...] + got_ref[...].astype(F32)).astype(BF16)


def sum_kernel(place_ref, got_ref, keep_ref, send_ref):
    z_hi = place_ref[3]
    beside = z_hi + 1 - 2 * lax.rem(z_hi, 2)

    def summed(block):
        total = got_ref[block, 0].astype(F32)
        for y in range(1, 4):
            total += got_ref[block, y].astype(F32)
        return total

    for index in range(2):
        send_ref[index] = summed(beside + index * (3 - 2 * beside)).astype(BF16)
        keep_ref[index] = summed(z_hi + index * (3 - 2 * z_hi))


def pair_kernel(keep_ref, got_ref, own_ref, send_ref):
    own_ref[...] = keep_ref[0] + got_ref[0].astype(F32)
    send_ref[...] = keep_ref[1] + got_ref[1].astype(F32)


def last_kernel(own_ref, got_ref, out_ref):
    out_ref[...] = (own_ref[...] + got_ref[...]).T


def pack_rows_kernel(place_ref, own_ref, a_ref, b_ref, c_ref, out_ref):
    other = 1 - place_ref[2]
    out_ref[0] = own_ref[0, other]
    for step, ref in enumerate((a_ref, b_ref, c_ref)):
        out_ref[step + 1] = ref[other]


def assemble_kernel(place_ref, own_ref, a_ref, b_ref, c_ref, far_ref, q_ref, k_ref):
    x, z_lo = place_ref[0], place_ref[2]

    def put(rows, z, step):
        src = z * 4 + lax.rem(x + 4 - step, 4)
        q_ref[:, pl.ds(pl.multiple_of(src * 2 * HD, 2 * HD), 2 * HD)] = rows[:, : 2 * HD]
        k_ref[:, pl.ds(pl.multiple_of(src * HD, HD), HD)] = rows[:, 2 * HD :]

    put(own_ref[0, z_lo], z_lo, 0)
    for step, ref in enumerate((a_ref, b_ref, c_ref)):
        put(ref[z_lo], z_lo, step + 1)
    for step in range(4):
        put(far_ref[step], 1 - z_lo, step)


def call(
    kernel, shapes, *args, place=None, after=(), behind=(), anywhere=False, flops=0,
    nbytes=1 << 20, scratch=(),
):
    space = pltpu.MemorySpace.HBM if anywhere else pltpu.VMEM
    specs = [pl.BlockSpec(memory_space=space)] * len(args)
    shapes = list(shapes) if isinstance(shapes, (list, tuple)) else [shapes]
    out_specs = [pl.BlockSpec(memory_space=pltpu.VMEM)] * len(shapes)
    if place is not None:
        args = (place,) + args
        specs = [pl.BlockSpec(memory_space=pltpu.SMEM)] + specs
    n_in, n_out, n_after, n_behind = len(args), len(shapes), len(after), len(behind)
    args += tuple(after) + tuple(behind)
    specs += [pl.BlockSpec(memory_space=pl.ANY)] * (n_after + n_behind)
    shapes += [jax.ShapeDtypeStruct(x.shape, x.dtype) for x in behind]
    out_specs += [pl.BlockSpec(memory_space=pl.ANY)] * n_behind
    first_out = n_in + n_after + n_behind

    def body(*refs):
        outs = refs[first_out : first_out + n_out]
        kernel(*refs[:n_in], *outs, *refs[first_out + n_out + n_behind :])

    outs = pl.pallas_call(
        body,
        out_shape=shapes,
        in_specs=specs,
        out_specs=out_specs,
        scratch_shapes=list(scratch),
        input_output_aliases={n_in + n_after + i: n_out + i for i in range(n_behind)},
        compiler_params=params(),
        cost_estimate=pl.CostEstimate(flops=flops, bytes_accessed=nbytes, transcendentals=0),
    )(*args)
    return outs if len(outs) > 1 else outs[0]


def shape_of(*dims, dtype=BF16):
    return jax.ShapeDtypeStruct(dims, dtype)


def shift(array, axis, size, by):
    return lax.ppermute(array, axis, [(i, (i + by) % size) for i in range(size)])


def on_device(queries, key_heads, value_heads, grad_out, features):
    q, k, v = queries[0], key_heads[0], value_heads[0]
    length = q.shape[0]
    seq = ("z_lo", "x")
    place = jnp.stack([lax.axis_index(a) for a in ("x", "core", "z_lo", "z_hi")]).astype(jnp.int32)
    tok = grad_out.shape[1]
    width = features.shape[2] // 4

    cot_parts = call(pack_cot_kernel, shape_of(8, tok, 2 * HD), grad_out[0])
    cot = lax.all_to_all(cot_parts, seq, 0, 0).reshape(length, 2 * HD)

    parts = call(
        pack_features_kernel, [shape_of(tok, width)] * 4, features[0], place=place, nbytes=2 << 20
    )
    near = [shift(parts[step], "x", 4, step) for step in range(1, 4)]
    far = shift(parts[0], "z_lo", 2, 1)

    probs = probs_of(q, k)
    dv = call(
        value_kernel, shape_of(HD, length), probs, cot, after=[far], flops=1 << 29, nbytes=5 << 20
    )
    first = call(gate_kernel, [], after=[dv], behind=near[:1])
    rest = call(join_kernel, shape_of(2, tok, width), *near[1:], after=[dv], nbytes=2 << 20)
    near = [parts[0], first, *near[1:]]
    far = [far, shift(first, "z_lo", 2, 1), shift(rest, "z_lo", 2, 1)]

    values = [dv] + [shift(dv, "x", 4, -step) for step in range(1, 4)]

    moved = grads_of(place, probs, q, k, v, cot, dv)
    half = length // 2
    part, other = call(
        near_kernel,
        [shape_of(4 * HD, width, dtype=F32), shape_of(4 * HD, half)],
        *values, *near,
        place=place,
        after=[moved],
        flops=0,
        nbytes=0,
        scratch=[pltpu.VMEM((4 * HD, half), BF16), pltpu.VMEM((half, width), BF16)],
    )
    keep, send = call(
        far_kernel,
        [shape_of(4, 4, HD, HD, dtype=F32), shape_of(4, 4, HD, HD)],
        part, other, *far,
        place=place,
        flops=LONG,
        nbytes=5 << 20,
        scratch=[pltpu.VMEM((half, width), BF16)],
    )
    got_x = [shift(moved[step], "x", 4, step) for step in range(1, 4)]
    send = call(gate_kernel, [], after=got_x, behind=[send])
    both = call(add_kernel, shape_of(4, 4, HD, HD), keep, shift(send, "core", 2, 1))
    over_y = lax.all_to_all(both.reshape(16, HD, HD), ("x", "y"), 0, 0).reshape(4, 4, HD, HD)
    keep, send = call(
        sum_kernel,
        [shape_of(2, HD, HD, dtype=F32), shape_of(2, HD, HD)],
        over_y,
        place=place,
        flops=LONG,
    )
    got = lax.ppermute(send, "z_hi", [(z, z ^ 1) for z in range(4)])
    own, send = call(pair_kernel, [shape_of(HD, HD, dtype=F32)] * 2, keep, got)
    got = lax.ppermute(send, "z_hi", [(z, 3 - z) for z in range(4)])
    packed = call(
        pack_rows_kernel, shape_of(4, tok, 3 * HD), moved, *got_x, place=place, after=[both]
    )
    got_z = shift(packed, "z_lo", 2, 1)
    query_grad, key_grad = call(
        assemble_kernel,
        (shape_of(tok, 16 * HD), shape_of(tok, 8 * HD)),
        moved, *got_x, got_z,
        place=place,
        after=[own],
    )
    weight_grad = call(last_kernel, shape_of(HD, HD, dtype=F32), own, got)
    return query_grad[None], key_grad[None], weight_grad


def solution(mesh):
    fine = Mesh(mesh.devices.reshape(2, 4, 4, 4, 2), ("z_lo", "x", "z_hi", "y", "core"))
    seq, dp = ("z_lo", "x"), ("z_hi", "y", "core")
    return jax.shard_map(
        on_device,
        mesh=fine,
        in_specs=(P(dp, None, seq), P(dp, None, seq), P(dp, None, seq), P(dp, seq, None), P(dp, seq, None)),
        out_specs=(P(dp, seq, None), P(dp, seq, None), P(dp, seq)),
        check_vma=False,
    )
```

```python
import math

import jax
import jax.numpy as jnp
from jax import lax
from jax.experimental import pallas as pl
from jax.experimental.pallas import tpu as pltpu
from jax.sharding import Mesh
from jax.sharding import PartitionSpec as P

HD = 128
BLK = 256
NN = (((1,), (0,)), ((), ()))
NT = (((1,), (1,)), ((), ()))
F32 = jnp.float32
BF16 = jnp.bfloat16
VMEM_LIMIT = 24 * 1024 * 1024
LONG = 1 << 35


def dot(a, b, dims):
    return lax.dot_general(a, b, dims, preferred_element_type=F32)


def packed_row(start):
    block = start // BLK
    return block * (block + 1) // 2 * BLK


def probs_kernel(q_ref, k_ref, p_ref, buf_ref, sems):
    length = k_ref.shape[0]
    inv_root = 1.0 / math.sqrt(HD)
    shape = (BLK, BLK)
    keep = lax.broadcasted_iota(jnp.int32, shape, 0) <= lax.broadcasted_iota(jnp.int32, shape, 1)
    copies = []
    for head in range(2):
        for start in range(0, length, BLK):
            stop = start + BLK
            q_block = q_ref[start:stop, head * HD : (head + 1) * HD]
            scores = dot(k_ref[:stop], q_block, NT) * inv_root
            last = jnp.where(keep, scores[start:], -jnp.inf)
            if start:
                scores = jnp.concatenate([scores[:start], last], axis=0)
            else:
                scores = last
            weights = jnp.exp(scores - jnp.max(scores, axis=0, keepdims=True))
            scale = 1.0 / jnp.sum(weights, axis=0, keepdims=True)
            first = packed_row(start)
            buf_ref[head, first : first + stop] = (weights * scale).astype(BF16)
            part = (head, pl.ds(first, stop))
            copies.append(
                pltpu.make_async_copy(buf_ref.at[part], p_ref.at[part], sems.at[len(copies)])
            )
            copies[-1].start()
    for copy in copies:
        copy.wait()


def value_kernel(place_ref, p_ref, cot_ref, *refs):
    out_refs, dv_ref = refs[:4], refs[4]
    length = cot_ref.shape[0]
    for jstart in range(0, length, BLK):
        jstop = jstart + BLK
        total = jnp.zeros((BLK, HD), F32)
        for head in range(2):
            for start in range(jstart, length, BLK):
                first = packed_row(start) + jstart
                total += dot(
                    p_ref[head, first : first + BLK],
                    cot_ref[start : start + BLK, head * HD : (head + 1) * HD],
                    NN,
                )
        dv_ref[:, jstart:jstop] = total.T.astype(BF16)
    tok = length // 8
    for step, ref in enumerate(out_refs):
        x = lax.rem(place_ref[0] + step, 4)
        for z in range(2):
            start = pl.multiple_of((z * 4 + x) * tok, tok)
            ref[:, z * tok : (z + 1) * tok] = dv_ref[:, pl.ds(start, tok)]


def columns_kernel(place_ref, *refs):
    for step, ref in enumerate(refs[:4]):
        block = lax.rem(place_ref[0] + 4 - step, 4)
        refs[4][pl.ds(pl.multiple_of(block * HD, HD), HD), :] = ref[...]


def grads_kernel(place_ref, p_ref, q_ref, k_ref, v_ref, cot_ref, out_ref, kt_ref, dk_ref):
    length = k_ref.shape[0]
    tok = out_ref.shape[2]
    inv_root = 1.0 / math.sqrt(HD)
    kt_ref[...] = k_ref[...].T
    dk_ref[...] = jnp.zeros_like(dk_ref)

    def put(rows, first, cols):
        for part in range(rows.shape[0] // tok):
            block = first // tok + part
            step = lax.rem(block % 4 + 4 - place_ref[0], 4)
            out_ref[step, block // 4, :, cols] = rows[part * tok : (part + 1) * tok]

    for head in range(2):
        cols = slice(head * HD, (head + 1) * HD)
        for start in range(0, length, BLK):
            stop = start + BLK
            dprobs = dot(v_ref[:stop], cot_ref[start:stop, cols], NT)
            first = packed_row(start)
            probs = p_ref[head, first : first + stop].astype(F32)
            row_dot = jnp.sum(probs * dprobs, axis=0, keepdims=True) / jnp.sum(
                probs, axis=0, keepdims=True
            )
            score_grad = (probs * (dprobs - row_dot)).astype(BF16)
            dk_ref[:stop] += dot(score_grad, q_ref[start:stop, cols], NN)
            dq_t = dot(kt_ref[:, :stop], score_grad, NN) * inv_root
            put(dq_t.T.astype(BF16), start, cols)
    put((dk_ref[...] * inv_root).astype(BF16), 0, slice(2 * HD, 3 * HD))


def params():
    return pltpu.CompilerParams(vmem_limit_bytes=VMEM_LIMIT)


def in_hbm(array):
    return pltpu.with_memory_space_constraint(array, pltpu.HBM)


def probs_of(q, k):
    length = k.shape[0]
    rows = packed_row(length)
    vmem = pl.BlockSpec(memory_space=pltpu.VMEM)
    return pl.pallas_call(
        probs_kernel,
        in_specs=[vmem, vmem],
        out_specs=pl.BlockSpec(memory_space=pl.ANY),
        out_shape=pltpu.HBM((2, rows, BLK), BF16),
        scratch_shapes=[pltpu.VMEM((2, rows, BLK), BF16), pltpu.SemaphoreType.DMA((8,))],
        compiler_params=params(),
        cost_estimate=pl.CostEstimate(
            flops=LONG, bytes_accessed=5 << 20, transcendentals=length * length
        ),
    )(in_hbm(q), in_hbm(k))


def grads_of(place, probs, q, k, v, cot, after):
    length = cot.shape[0]
    return call(
        grads_kernel,
        shape_of(4, 2, length // 8, 3 * HD),
        probs, q, k, v, cot,
        place=place,
        after=[after],
        flops=LONG,
        nbytes=6 << 20,
        scratch=[pltpu.VMEM((HD, length), BF16), pltpu.VMEM((length, HD), F32)],
    )


def pack_cot_kernel(cot_ref, out_ref):
    for dest in range(8):
        out_ref[dest] = cot_ref[:, dest * 2 * HD : (dest + 1) * 2 * HD]


def pack_features_kernel(place_ref, f_ref, *out_refs):
    for step, ref in enumerate(out_refs):
        y = lax.rem(place_ref[4] + step, 4)
        for z in range(4):
            start = pl.multiple_of((z * 4 + y) * 2 * HD, 2 * HD)
            ref[:, z * 2 * HD : (z + 1) * 2 * HD] = f_ref[:, pl.ds(start, 2 * HD)]


def join_kernel(*refs):
    for index, ref in enumerate(refs[:-1]):
        refs[-1][index] = ref[...]


def gate_kernel():
    pass


def near_kernel(place_ref, *refs):
    v_refs, f_refs, (part_ref, other_ref, v_ref, f_ref) = refs[:4], refs[4:8], refs[8:]
    y, z_lo = place_ref[4], place_ref[2]
    tok = f_refs[0].shape[0]
    for step, ref in enumerate(v_refs):
        cols = pl.ds(pl.multiple_of(lax.rem(y + step, 4) * tok, tok), tok)
        v_ref[:, cols] = ref[:, pl.ds(pl.multiple_of(z_lo * tok, tok), tok)]
        other_ref[:, cols] = ref[:, pl.ds(pl.multiple_of((1 - z_lo) * tok, tok), tok)]
    for step, ref in enumerate(f_refs):
        block = lax.rem(y + 4 - step, 4)
        f_ref[pl.ds(pl.multiple_of(block * tok, tok), tok), :] = ref[...]
    for z in range(4):
        cols = slice(z * 2 * HD, (z + 1) * 2 * HD)
        part_ref[:, cols] = dot(v_ref[...], f_ref[:, cols], NN)


def far_kernel(place_ref, part_ref, v_ref, *refs):
    own_ref, rest_ref, keep_ref, send_ref, f_ref = refs
    y, core = place_ref[4], place_ref[1]
    tok = own_ref.shape[0]
    for step, ref in enumerate((own_ref, *(rest_ref.at[i] for i in range(3)))):
        block = lax.rem(y + 4 - step, 4)
        f_ref[pl.ds(pl.multiple_of(block * tok, tok), tok), :] = ref[...]
    for z in range(4):
        cols = slice(z * 2 * HD, (z + 1) * 2 * HD)
        total = part_ref[:, cols] + dot(v_ref[...], f_ref[:, cols], NN)
        mine = jnp.where(core == 0, total[:, :HD], total[:, HD:])
        other = jnp.where(core == 0, total[:, HD:], total[:, :HD]).astype(BF16)
        for e in range(4):
            keep_ref[e, z] = mine[e * HD : (e + 1) * HD]
            send_ref[e, z] = other[e * HD : (e + 1) * HD]


def add_kernel(keep_ref, got_ref, out_ref):
    out_ref[...] = (keep_ref[...] + got_ref[...].astype(F32)).astype(BF16)


def sum_kernel(place_ref, got_ref, keep_ref, send_ref):
    z_hi = place_ref[3]
    beside = z_hi + 1 - 2 * lax.rem(z_hi, 2)

    def summed(block):
        total = got_ref[0, block].astype(F32)
        for x in range(1, 4):
            total += got_ref[x, block].astype(F32)
        return total

    for index in range(2):
        send_ref[index] = summed(beside + index * (3 - 2 * beside)).astype(BF16)
        keep_ref[index] = summed(z_hi + index * (3 - 2 * z_hi))


def pair_kernel(keep_ref, got_ref, own_ref, send_ref):
    own_ref[...] = keep_ref[0] + got_ref[0].astype(F32)
    send_ref[...] = keep_ref[1] + got_ref[1].astype(F32)


def last_kernel(own_ref, got_ref, out_ref):
    out_ref[...] = (own_ref[...] + got_ref[...]).T


def pack_rows_kernel(place_ref, own_ref, a_ref, b_ref, c_ref, out_ref):
    other = 1 - place_ref[2]
    out_ref[0] = own_ref[0, other]
    for step, ref in enumerate((a_ref, b_ref, c_ref)):
        out_ref[step + 1] = ref[other]


def assemble_kernel(place_ref, own_ref, a_ref, b_ref, c_ref, far_ref, q_ref, k_ref):
    x, z_lo = place_ref[0], place_ref[2]

    def put(rows, z, step):
        src = z * 4 + lax.rem(x + 4 - step, 4)
        q_ref[:, pl.ds(pl.multiple_of(src * 2 * HD, 2 * HD), 2 * HD)] = rows[:, : 2 * HD]
        k_ref[:, pl.ds(pl.multiple_of(src * HD, HD), HD)] = rows[:, 2 * HD :]

    put(own_ref[0, z_lo], z_lo, 0)
    for step, ref in enumerate((a_ref, b_ref, c_ref)):
        put(ref[z_lo], z_lo, step + 1)
    for step in range(4):
        put(far_ref[step], 1 - z_lo, step)


def call(
    kernel, shapes, *args, place=None, after=(), behind=(), anywhere=False, flops=0,
    nbytes=1 << 20, scratch=(),
):
    space = pltpu.MemorySpace.HBM if anywhere else pltpu.VMEM
    specs = [pl.BlockSpec(memory_space=space)] * len(args)
    shapes = list(shapes) if isinstance(shapes, (list, tuple)) else [shapes]
    out_specs = [pl.BlockSpec(memory_space=pltpu.VMEM)] * len(shapes)
    if place is not None:
        args = (place,) + args
        specs = [pl.BlockSpec(memory_space=pltpu.SMEM)] + specs
    n_in, n_out, n_after, n_behind = len(args), len(shapes), len(after), len(behind)
    args += tuple(after) + tuple(behind)
    specs += [pl.BlockSpec(memory_space=pl.ANY)] * (n_after + n_behind)
    shapes += [jax.ShapeDtypeStruct(x.shape, x.dtype) for x in behind]
    out_specs += [pl.BlockSpec(memory_space=pl.ANY)] * n_behind
    first_out = n_in + n_after + n_behind

    def body(*refs):
        outs = refs[first_out : first_out + n_out]
        kernel(*refs[:n_in], *outs, *refs[first_out + n_out + n_behind :])

    outs = pl.pallas_call(
        body,
        out_shape=shapes,
        in_specs=specs,
        out_specs=out_specs,
        scratch_shapes=list(scratch),
        input_output_aliases={n_in + n_after + i: n_out + i for i in range(n_behind)},
        compiler_params=params(),
        cost_estimate=pl.CostEstimate(flops=flops, bytes_accessed=nbytes, transcendentals=0),
    )(*args)
    return outs if len(outs) > 1 else outs[0]


def shape_of(*dims, dtype=BF16):
    return jax.ShapeDtypeStruct(dims, dtype)


def shift(array, axis, size, by):
    return lax.ppermute(array, axis, [(i, (i + by) % size) for i in range(size)])


def on_device(queries, key_heads, value_heads, grad_out, features):
    q, k, v = queries[0], key_heads[0], value_heads[0]
    length = q.shape[0]
    seq = ("z_lo", "x")
    place = jnp.stack([lax.axis_index(a) for a in ("x", "core", "z_lo", "z_hi", "y")]).astype(jnp.int32)
    tok = grad_out.shape[1]
    width = features.shape[2] // 4

    cot_parts = call(pack_cot_kernel, shape_of(8, tok, 2 * HD), grad_out[0])
    cot = lax.all_to_all(cot_parts, seq, 0, 0).reshape(length, 2 * HD)

    parts = call(
        pack_features_kernel,
        [shape_of(tok, width)] * 4,
        features[0],
        place=place,
        after=[cot_parts],
        nbytes=2 << 20,
    )
    near = [shift(parts[step], "y", 4, step) for step in range(1, 4)]
    far = shift(parts[0], "z_lo", 2, 1)

    probs = probs_of(q, k)
    pieces = call(
        value_kernel,
        [shape_of(HD, 2 * tok)] * 4,
        probs, cot,
        place=place,
        flops=1 << 29,
        nbytes=5 << 20,
        scratch=[pltpu.VMEM((HD, length), BF16)],
    )
    dv = pieces[0]
    pieces = [dv] + [shift(pieces[step], "x", 4, step) for step in range(1, 4)]
    columns = call(columns_kernel, shape_of(4 * HD, 2 * tok), *pieces, place=place)
    rest = call(join_kernel, shape_of(3, tok, width), *near, after=[dv, far], nbytes=2 << 20)
    near = [parts[0], *near]
    far = [far, shift(rest, "z_lo", 2, 1)]

    values = [columns] + [shift(columns, "y", 4, -step) for step in range(1, 4)]

    moved = grads_of(place, probs, q, k, v, cot, dv)
    half = length // 2
    part, other = call(
        near_kernel,
        [shape_of(4 * HD, width, dtype=F32), shape_of(4 * HD, half)],
        *values, *near,
        place=place,
        after=[moved],
        flops=0,
        nbytes=0,
        scratch=[pltpu.VMEM((4 * HD, half), BF16), pltpu.VMEM((half, width), BF16)],
    )
    keep, send = call(
        far_kernel,
        [shape_of(4, 4, HD, HD, dtype=F32), shape_of(4, 4, HD, HD)],
        part, other, *far,
        place=place,
        flops=LONG,
        nbytes=5 << 20,
        scratch=[pltpu.VMEM((half, width), BF16)],
    )
    got_x = [shift(moved[step], "x", 4, step) for step in range(1, 4)]
    send = call(gate_kernel, [], after=got_x, behind=[send])
    both = call(add_kernel, shape_of(4, 4, HD, HD), keep, shift(send, "core", 2, 1))
    over_x = lax.all_to_all(both, "x", 0, 0)
    keep, send = call(
        sum_kernel,
        [shape_of(2, HD, HD, dtype=F32), shape_of(2, HD, HD)],
        over_x,
        place=place,
        flops=LONG,
    )
    got = lax.ppermute(send, "z_hi", [(z, z ^ 1) for z in range(4)])
    own, send = call(pair_kernel, [shape_of(HD, HD, dtype=F32)] * 2, keep, got)
    got = lax.ppermute(send, "z_hi", [(z, 3 - z) for z in range(4)])
    packed = call(
        pack_rows_kernel, shape_of(4, tok, 3 * HD), moved, *got_x, place=place, after=[both]
    )
    got_z = shift(packed, "z_lo", 2, 1)
    query_grad, key_grad = call(
        assemble_kernel,
        (shape_of(tok, 16 * HD), shape_of(tok, 8 * HD)),
        moved, *got_x, got_z,
        place=place,
        after=[own],
    )
    weight_grad = call(last_kernel, shape_of(HD, HD, dtype=F32), own, got)
    return query_grad[None], key_grad[None], weight_grad


def solution(mesh):
    fine = Mesh(mesh.devices.reshape(2, 4, 4, 4, 2), ("z_lo", "x", "z_hi", "y", "core"))
    seq, dp = ("z_lo", "x"), ("z_hi", "y", "core")
    return jax.shard_map(
        on_device,
        mesh=fine,
        in_specs=(P(dp, None, seq), P(dp, None, seq), P(dp, None, seq), P(dp, seq, None), P(dp, seq, None)),
        out_specs=(P(dp, seq, None), P(dp, seq, None), P(dp, seq)),
        check_vma=False,
    )
```

```python
import math

import jax
import jax.numpy as jnp
from jax import lax
from jax.experimental import pallas as pl
from jax.experimental.pallas import tpu as pltpu
from jax.sharding import Mesh
from jax.sharding import PartitionSpec as P

HD = 128
BLK = 256
NN = (((1,), (0,)), ((), ()))
NT = (((1,), (1,)), ((), ()))
F32 = jnp.float32
BF16 = jnp.bfloat16
VMEM_LIMIT = 24 * 1024 * 1024
LONG = 1 << 35


def dot(a, b, dims):
    return lax.dot_general(a, b, dims, preferred_element_type=F32)


def packed_row(start):
    block = start // BLK
    return block * (block + 1) // 2 * BLK


def probs_kernel(q_ref, k_ref, p_ref, buf_ref, sems):
    length = k_ref.shape[0]
    inv_root = 1.0 / math.sqrt(HD)
    shape = (BLK, BLK)
    keep = lax.broadcasted_iota(jnp.int32, shape, 0) <= lax.broadcasted_iota(jnp.int32, shape, 1)
    copies = []
    for head in range(2):
        for start in range(0, length, BLK):
            stop = start + BLK
            q_block = q_ref[start:stop, head * HD : (head + 1) * HD]
            scores = dot(k_ref[:stop], q_block, NT) * inv_root
            last = jnp.where(keep, scores[start:], -jnp.inf)
            if start:
                scores = jnp.concatenate([scores[:start], last], axis=0)
            else:
                scores = last
            weights = jnp.exp(scores - jnp.max(scores, axis=0, keepdims=True))
            scale = 1.0 / jnp.sum(weights, axis=0, keepdims=True)
            first = packed_row(start)
            buf_ref[head, first : first + stop] = (weights * scale).astype(BF16)
            part = (head, pl.ds(first, stop))
            copies.append(
                pltpu.make_async_copy(buf_ref.at[part], p_ref.at[part], sems.at[len(copies)])
            )
            copies[-1].start()
    for copy in copies:
        copy.wait()


def value_kernel(place_ref, p_ref, cot_ref, *refs):
    out_refs, dv_ref = refs[:4], refs[4]
    length = cot_ref.shape[0]
    for jstart in range(0, length, BLK):
        jstop = jstart + BLK
        total = jnp.zeros((BLK, HD), F32)
        for head in range(2):
            for start in range(jstart, length, BLK):
                first = packed_row(start) + jstart
                total += dot(
                    p_ref[head, first : first + BLK],
                    cot_ref[start : start + BLK, head * HD : (head + 1) * HD],
                    NN,
                )
        dv_ref[:, jstart:jstop] = total.T.astype(BF16)
    tok = length // 8
    for step, ref in enumerate(out_refs):
        x = lax.rem(place_ref[0] + step, 4)
        for z in range(2):
            start = pl.multiple_of((z * 4 + x) * tok, tok)
            ref[:, z * tok : (z + 1) * tok] = dv_ref[:, pl.ds(start, tok)]


def columns_kernel(place_ref, *refs):
    for step, ref in enumerate(refs[:4]):
        block = lax.rem(place_ref[0] + 4 - step, 4)
        refs[4][pl.ds(pl.multiple_of(block * HD, HD), HD), :] = ref[...]


def grads_kernel(place_ref, p_ref, q_ref, k_ref, v_ref, cot_ref, out_ref, kt_ref, dk_ref):
    length = k_ref.shape[0]
    tok = out_ref.shape[2]
    inv_root = 1.0 / math.sqrt(HD)
    kt_ref[...] = k_ref[...].T
    dk_ref[...] = jnp.zeros_like(dk_ref)

    def put(rows, first, cols):
        for part in range(rows.shape[0] // tok):
            block = first // tok + part
            step = lax.rem(block % 4 + 4 - place_ref[0], 4)
            out_ref[step, block // 4, :, cols] = rows[part * tok : (part + 1) * tok]

    for head in range(2):
        cols = slice(head * HD, (head + 1) * HD)
        for start in range(0, length, BLK):
            stop = start + BLK
            dprobs = dot(v_ref[:stop], cot_ref[start:stop, cols], NT)
            first = packed_row(start)
            probs = p_ref[head, first : first + stop].astype(F32)
            row_dot = jnp.sum(probs * dprobs, axis=0, keepdims=True) / jnp.sum(
                probs, axis=0, keepdims=True
            )
            score_grad = (probs * (dprobs - row_dot)).astype(BF16)
            dk_ref[:stop] += dot(score_grad, q_ref[start:stop, cols], NN)
            dq_t = dot(kt_ref[:, :stop], score_grad, NN) * inv_root
            put(dq_t.T.astype(BF16), start, cols)
    put((dk_ref[...] * inv_root).astype(BF16), 0, slice(2 * HD, 3 * HD))


def params():
    return pltpu.CompilerParams(vmem_limit_bytes=VMEM_LIMIT)


def in_hbm(array):
    return pltpu.with_memory_space_constraint(array, pltpu.HBM)


def probs_of(q, k):
    length = k.shape[0]
    rows = packed_row(length)
    vmem = pl.BlockSpec(memory_space=pltpu.VMEM)
    return pl.pallas_call(
        probs_kernel,
        in_specs=[vmem, vmem],
        out_specs=pl.BlockSpec(memory_space=pl.ANY),
        out_shape=pltpu.HBM((2, rows, BLK), BF16),
        scratch_shapes=[pltpu.VMEM((2, rows, BLK), BF16), pltpu.SemaphoreType.DMA((8,))],
        compiler_params=params(),
        cost_estimate=pl.CostEstimate(
            flops=LONG, bytes_accessed=5 << 20, transcendentals=length * length
        ),
    )(in_hbm(q), in_hbm(k))


def grads_of(place, probs, q, k, v, cot, after):
    length = cot.shape[0]
    return call(
        grads_kernel,
        shape_of(4, 2, length // 8, 3 * HD),
        probs, q, k, v, cot,
        place=place,
        after=[after],
        flops=LONG,
        nbytes=6 << 20,
        scratch=[pltpu.VMEM((HD, length), BF16), pltpu.VMEM((length, HD), F32)],
    )


def pack_cot_kernel(cot_ref, out_ref):
    for dest in range(8):
        out_ref[dest] = cot_ref[:, dest * 2 * HD : (dest + 1) * 2 * HD]


def pack_features_kernel(place_ref, f_ref, *out_refs):
    for step, ref in enumerate(out_refs):
        y = lax.rem(place_ref[4] + step, 4)
        for z in range(4):
            start = pl.multiple_of((z * 4 + y) * 2 * HD, 2 * HD)
            ref[:, z * 2 * HD : (z + 1) * 2 * HD] = f_ref[:, pl.ds(start, 2 * HD)]


def join_kernel(*refs):
    for index, ref in enumerate(refs[:-1]):
        refs[-1][index] = ref[...]


def gate_kernel():
    pass


def near_kernel(place_ref, *refs):
    v_refs, f_refs, (part_ref, other_ref, v_ref, f_ref) = refs[:4], refs[4:8], refs[8:]
    y, z_lo = place_ref[4], place_ref[2]
    tok = f_refs[0].shape[0]
    for step, ref in enumerate(v_refs):
        cols = pl.ds(pl.multiple_of(lax.rem(y + step, 4) * tok, tok), tok)
        v_ref[:, cols] = ref[:, pl.ds(pl.multiple_of(z_lo * tok, tok), tok)]
        other_ref[:, cols] = ref[:, pl.ds(pl.multiple_of((1 - z_lo) * tok, tok), tok)]
    for step, ref in enumerate(f_refs):
        block = lax.rem(y + 4 - step, 4)
        f_ref[pl.ds(pl.multiple_of(block * tok, tok), tok), :] = ref[...]
    for z in range(4):
        cols = slice(z * 2 * HD, (z + 1) * 2 * HD)
        part_ref[:, cols] = dot(v_ref[...], f_ref[:, cols], NN)


def far_kernel(place_ref, part_ref, v_ref, *refs):
    own_ref, rest_ref, keep_ref, send_ref, f_ref = refs
    y, core = place_ref[4], place_ref[1]
    tok = own_ref.shape[0]
    for step, ref in enumerate((own_ref, *(rest_ref.at[i] for i in range(3)))):
        block = lax.rem(y + 4 - step, 4)
        f_ref[pl.ds(pl.multiple_of(block * tok, tok), tok), :] = ref[...]
    for z in range(4):
        cols = slice(z * 2 * HD, (z + 1) * 2 * HD)
        total = part_ref[:, cols] + dot(v_ref[...], f_ref[:, cols], NN)
        mine = jnp.where(core == 0, total[:, :HD], total[:, HD:])
        other = jnp.where(core == 0, total[:, HD:], total[:, :HD]).astype(BF16)
        for e in range(4):
            keep_ref[e, z] = mine[e * HD : (e + 1) * HD]
            send_ref[e, z] = other[e * HD : (e + 1) * HD]


def add_kernel(place_ref, keep_ref, got_ref, *out_refs):
    for step, ref in enumerate(out_refs):
        e = lax.rem(place_ref[0] + step, 4)
        ref[...] = (keep_ref[e] + got_ref[e].astype(F32)).astype(BF16)


def sum_kernel(place_ref, *refs):
    got_refs, (keep_ref, send_ref) = refs[:4], refs[4:]
    z_hi = place_ref[3]
    beside = z_hi + 1 - 2 * lax.rem(z_hi, 2)

    def summed(block):
        total = got_refs[0][block].astype(F32)
        for ref in got_refs[1:]:
            total += ref[block].astype(F32)
        return total

    for index in range(2):
        send_ref[index] = summed(beside + index * (3 - 2 * beside)).astype(BF16)
        keep_ref[index] = summed(z_hi + index * (3 - 2 * z_hi))


def pair_kernel(keep_ref, got_ref, own_ref, send_ref):
    own_ref[...] = keep_ref[0] + got_ref[0].astype(F32)
    send_ref[...] = keep_ref[1] + got_ref[1].astype(F32)


def last_kernel(own_ref, got_ref, out_ref):
    out_ref[...] = (own_ref[...] + got_ref[...]).T


def pack_rows_kernel(place_ref, own_ref, a_ref, b_ref, c_ref, out_ref):
    other = 1 - place_ref[2]
    out_ref[0] = own_ref[0, other]
    for step, ref in enumerate((a_ref, b_ref, c_ref)):
        out_ref[step + 1] = ref[other]


def assemble_kernel(place_ref, own_ref, a_ref, b_ref, c_ref, far_ref, q_ref, k_ref, done_ref):
    done_ref[...] = jnp.zeros_like(done_ref)
    x, z_lo = place_ref[0], place_ref[2]

    def put(rows, z, step):
        src = z * 4 + lax.rem(x + 4 - step, 4)
        q_ref[:, pl.ds(pl.multiple_of(src * 2 * HD, 2 * HD), 2 * HD)] = rows[:, : 2 * HD]
        k_ref[:, pl.ds(pl.multiple_of(src * HD, HD), HD)] = rows[:, 2 * HD :]

    put(own_ref[0, z_lo], z_lo, 0)
    for step, ref in enumerate((a_ref, b_ref, c_ref)):
        put(ref[z_lo], z_lo, step + 1)
    for step in range(4):
        put(far_ref[step], 1 - z_lo, step)


def call(
    kernel, shapes, *args, place=None, after=(), behind=(), anywhere=False, flops=0,
    nbytes=1 << 20, scratch=(),
):
    space = pltpu.MemorySpace.HBM if anywhere else pltpu.VMEM
    specs = [pl.BlockSpec(memory_space=space)] * len(args)
    shapes = list(shapes) if isinstance(shapes, (list, tuple)) else [shapes]
    out_specs = [pl.BlockSpec(memory_space=pltpu.VMEM)] * len(shapes)
    if place is not None:
        args = (place,) + args
        specs = [pl.BlockSpec(memory_space=pltpu.SMEM)] + specs
    n_in, n_out, n_after, n_behind = len(args), len(shapes), len(after), len(behind)
    args += tuple(after) + tuple(behind)
    specs += [pl.BlockSpec(memory_space=pl.ANY)] * (n_after + n_behind)
    shapes += [jax.ShapeDtypeStruct(x.shape, x.dtype) for x in behind]
    out_specs += [pl.BlockSpec(memory_space=pl.ANY)] * n_behind
    first_out = n_in + n_after + n_behind

    def body(*refs):
        outs = refs[first_out : first_out + n_out]
        kernel(*refs[:n_in], *outs, *refs[first_out + n_out + n_behind :])

    outs = pl.pallas_call(
        body,
        out_shape=shapes,
        in_specs=specs,
        out_specs=out_specs,
        scratch_shapes=list(scratch),
        input_output_aliases={n_in + n_after + i: n_out + i for i in range(n_behind)},
        compiler_params=params(),
        cost_estimate=pl.CostEstimate(flops=flops, bytes_accessed=nbytes, transcendentals=0),
    )(*args)
    return outs if len(outs) > 1 else outs[0]


def shape_of(*dims, dtype=BF16):
    return jax.ShapeDtypeStruct(dims, dtype)


def shift(array, axis, size, by):
    return lax.ppermute(array, axis, [(i, (i + by) % size) for i in range(size)])


def on_device(queries, key_heads, value_heads, grad_out, features):
    q, k, v = queries[0], key_heads[0], value_heads[0]
    length = q.shape[0]
    seq = ("z_lo", "x")
    place = jnp.stack([lax.axis_index(a) for a in ("x", "core", "z_lo", "z_hi", "y")]).astype(jnp.int32)
    tok = grad_out.shape[1]
    width = features.shape[2] // 4

    cot_parts = call(pack_cot_kernel, shape_of(8, tok, 2 * HD), grad_out[0])
    cot = lax.all_to_all(cot_parts, seq, 0, 0).reshape(length, 2 * HD)

    parts = call(
        pack_features_kernel,
        [shape_of(tok, width)] * 4,
        features[0],
        place=place,
        after=[cot_parts],
        nbytes=2 << 20,
    )
    near = [shift(parts[step], "y", 4, step) for step in range(1, 4)]
    far = shift(parts[0], "z_lo", 2, 1)

    probs = probs_of(q, k)
    pieces = call(
        value_kernel,
        [shape_of(HD, 2 * tok)] * 4,
        probs, cot,
        place=place,
        flops=1 << 29,
        nbytes=5 << 20,
        scratch=[pltpu.VMEM((HD, length), BF16)],
    )
    dv = pieces[0]
    pieces = [dv] + [shift(pieces[step], "x", 4, step) for step in range(1, 4)]
    columns = call(columns_kernel, shape_of(4 * HD, 2 * tok), *pieces, place=place)
    rest = call(join_kernel, shape_of(3, tok, width), *near, after=[dv, far], nbytes=2 << 20)
    near = [parts[0], *near]
    far = [far, shift(rest, "z_lo", 2, 1)]

    values = [columns] + [shift(columns, "y", 4, -step) for step in range(1, 4)]

    moved = grads_of(place, probs, q, k, v, cot, dv)
    half = length // 2
    part, other = call(
        near_kernel,
        [shape_of(4 * HD, width, dtype=F32), shape_of(4 * HD, half)],
        *values, *near,
        place=place,
        after=[moved],
        flops=0,
        nbytes=0,
        scratch=[pltpu.VMEM((4 * HD, half), BF16), pltpu.VMEM((half, width), BF16)],
    )
    keep, send = call(
        far_kernel,
        [shape_of(4, 4, HD, HD, dtype=F32), shape_of(4, 4, HD, HD)],
        part, other, *far,
        place=place,
        flops=LONG,
        nbytes=5 << 20,
        scratch=[pltpu.VMEM((half, width), BF16)],
    )
    got_x = [shift(moved[step], "x", 4, step) for step in range(1, 4)]
    send = call(gate_kernel, [], after=got_x, behind=[send])
    both = call(
        add_kernel, [shape_of(4, HD, HD)] * 4, keep, shift(send, "core", 2, 1), place=place
    )
    over_x = [both[0]] + [shift(both[step], "x", 4, step) for step in range(1, 4)]
    keep, send = call(
        sum_kernel,
        [shape_of(2, HD, HD, dtype=F32), shape_of(2, HD, HD)],
        *over_x,
        place=place,
        flops=LONG,
    )
    got = lax.ppermute(send, "z_hi", [(z, z ^ 1) for z in range(4)])
    own, send = call(pair_kernel, [shape_of(HD, HD, dtype=F32)] * 2, keep, got)
    got = lax.ppermute(send, "z_hi", [(z, 3 - z) for z in range(4)])
    packed = call(
        pack_rows_kernel, shape_of(4, tok, 3 * HD), moved, *got_x, place=place, after=[both[0]]
    )
    got_z = shift(packed, "z_lo", 2, 1)
    query_grad, key_grad, done = call(
        assemble_kernel,
        (shape_of(tok, 16 * HD), shape_of(tok, 8 * HD), shape_of(8, HD, dtype=F32)),
        moved, *got_x, got_z,
        place=place,
        after=[own],
    )
    weight_grad = call(last_kernel, shape_of(HD, HD, dtype=F32), own, got, after=[done])
    return query_grad[None], key_grad[None], weight_grad


def solution(mesh):
    fine = Mesh(mesh.devices.reshape(2, 4, 4, 4, 2), ("z_lo", "x", "z_hi", "y", "core"))
    seq, dp = ("z_lo", "x"), ("z_hi", "y", "core")
    return jax.shard_map(
        on_device,
        mesh=fine,
        in_specs=(P(dp, None, seq), P(dp, None, seq), P(dp, None, seq), P(dp, seq, None), P(dp, seq, None)),
        out_specs=(P(dp, seq, None), P(dp, seq, None), P(dp, seq)),
        check_vma=False,
    )
```

```python
import math

import jax
import jax.numpy as jnp
from jax import lax
from jax.experimental import pallas as pl
from jax.experimental.pallas import tpu as pltpu
from jax.sharding import Mesh
from jax.sharding import PartitionSpec as P

HD = 128
BLK = 256
NN = (((1,), (0,)), ((), ()))
NT = (((1,), (1,)), ((), ()))
F32 = jnp.float32
BF16 = jnp.bfloat16
VMEM_LIMIT = 24 * 1024 * 1024
LONG = 1 << 35


def dot(a, b, dims):
    return lax.dot_general(a, b, dims, preferred_element_type=F32)


def packed_row(start):
    block = start // BLK
    return block * (block + 1) // 2 * BLK


def probs_kernel(q_hbm, k_hbm, p_ref, buf_ref, q_ref, k_ref, sems, in_sems):
    length = k_ref.shape[0]
    inv_root = 1.0 / math.sqrt(HD)
    shape = (BLK, BLK)
    keep = lax.broadcasted_iota(jnp.int32, shape, 0) <= lax.broadcasted_iota(jnp.int32, shape, 1)
    loads = []
    for start in range(0, length, BLK):
        rows = pl.ds(start, BLK)
        for step, (src, dst) in enumerate(((k_hbm, k_ref), (q_hbm, q_ref))):
            sem = in_sems.at[start // BLK, step]
            loads.append(pltpu.make_async_copy(src.at[rows], dst.at[rows], sem))
            loads[-1].start()
    copies = []
    for start in range(0, length, BLK):
        stop = start + BLK
        loads.pop(0).wait()
        loads.pop(0).wait()
        for head in range(2):
            q_block = q_ref[start:stop, head * HD : (head + 1) * HD]
            scores = dot(k_ref[:stop], q_block, NT) * inv_root
            last = jnp.where(keep, scores[start:], -jnp.inf)
            if start:
                scores = jnp.concatenate([scores[:start], last], axis=0)
            else:
                scores = last
            weights = jnp.exp(scores - jnp.max(scores, axis=0, keepdims=True))
            scale = 1.0 / jnp.sum(weights, axis=0, keepdims=True)
            first = packed_row(start)
            buf_ref[head, first : first + stop] = (weights * scale).astype(BF16)
            part = (head, pl.ds(first, stop))
            copies.append(
                pltpu.make_async_copy(buf_ref.at[part], p_ref.at[part], sems.at[len(copies)])
            )
            copies[-1].start()
    for copy in copies:
        copy.wait()


def value_kernel(place_ref, p_ref, cot_ref, *refs):
    out_refs, dv_ref = refs[:4], refs[4]
    length = cot_ref.shape[0]
    for jstart in range(0, length, BLK):
        jstop = jstart + BLK
        total = jnp.zeros((BLK, HD), F32)
        for head in range(2):
            for start in range(jstart, length, BLK):
                first = packed_row(start) + jstart
                total += dot(
                    p_ref[head, first : first + BLK],
                    cot_ref[start : start + BLK, head * HD : (head + 1) * HD],
                    NN,
                )
        dv_ref[:, jstart:jstop] = total.T.astype(BF16)
    tok = length // 8
    for step, ref in enumerate(out_refs):
        x = lax.rem(place_ref[0] + step, 4)
        for z in range(2):
            start = pl.multiple_of((z * 4 + x) * tok, tok)
            ref[:, z * tok : (z + 1) * tok] = dv_ref[:, pl.ds(start, tok)]


def columns_kernel(place_ref, *refs):
    for step, ref in enumerate(refs[:4]):
        block = lax.rem(place_ref[0] + 4 - step, 4)
        refs[4][pl.ds(pl.multiple_of(block * HD, HD), HD), :] = ref[...]


def grads_kernel(place_ref, p_ref, q_ref, k_ref, v_ref, cot_ref, out_ref, kt_ref, dk_ref):
    length = k_ref.shape[0]
    tok = out_ref.shape[2]
    inv_root = 1.0 / math.sqrt(HD)
    kt_ref[...] = k_ref[...].T
    dk_ref[...] = jnp.zeros_like(dk_ref)

    def put(rows, first, cols):
        for part in range(rows.shape[0] // tok):
            block = first // tok + part
            step = lax.rem(block % 4 + 4 - place_ref[0], 4)
            out_ref[step, block // 4, :, cols] = rows[part * tok : (part + 1) * tok]

    for head in range(2):
        cols = slice(head * HD, (head + 1) * HD)
        for start in range(0, length, BLK):
            stop = start + BLK
            dprobs = dot(v_ref[:stop], cot_ref[start:stop, cols], NT)
            first = packed_row(start)
            probs = p_ref[head, first : first + stop].astype(F32)
            row_dot = jnp.sum(probs * dprobs, axis=0, keepdims=True) / jnp.sum(
                probs, axis=0, keepdims=True
            )
            score_grad = (probs * (dprobs - row_dot)).astype(BF16)
            dk_ref[:stop] += dot(score_grad, q_ref[start:stop, cols], NN)
            dq_t = dot(kt_ref[:, :stop], score_grad, NN) * inv_root
            put(dq_t.T.astype(BF16), start, cols)
    put((dk_ref[...] * inv_root).astype(BF16), 0, slice(2 * HD, 3 * HD))


def params():
    return pltpu.CompilerParams(vmem_limit_bytes=VMEM_LIMIT)


def in_hbm(array):
    return pltpu.with_memory_space_constraint(array, pltpu.HBM)


def probs_of(q, k):
    length = k.shape[0]
    rows = packed_row(length)
    return pl.pallas_call(
        probs_kernel,
        in_specs=[pl.BlockSpec(memory_space=pl.ANY)] * 2,
        out_specs=pl.BlockSpec(memory_space=pl.ANY),
        out_shape=pltpu.HBM((2, rows, BLK), BF16),
        scratch_shapes=[
            pltpu.VMEM((2, rows, BLK), BF16),
            pltpu.VMEM((length, 2 * HD), BF16),
            pltpu.VMEM((length, HD), BF16),
            pltpu.SemaphoreType.DMA((8,)),
            pltpu.SemaphoreType.DMA((length // BLK, 2)),
        ],
        compiler_params=params(),
        cost_estimate=pl.CostEstimate(
            flops=LONG, bytes_accessed=5 << 20, transcendentals=length * length
        ),
    )(in_hbm(q), in_hbm(k))


def grads_of(place, probs, q, k, v, cot, after):
    length = cot.shape[0]
    return call(
        grads_kernel,
        shape_of(4, 2, length // 8, 3 * HD),
        probs, q, k, v, cot,
        place=place,
        after=[after],
        flops=LONG,
        nbytes=6 << 20,
        scratch=[pltpu.VMEM((HD, length), BF16), pltpu.VMEM((length, HD), F32)],
    )


def pack_cot_kernel(cot_ref, out_ref):
    for dest in range(8):
        out_ref[dest] = cot_ref[:, dest * 2 * HD : (dest + 1) * 2 * HD]


def pack_features_kernel(place_ref, f_ref, *out_refs):
    for step, ref in enumerate(out_refs):
        y = lax.rem(place_ref[4] + step, 4)
        for z in range(4):
            start = pl.multiple_of((z * 4 + y) * 2 * HD, 2 * HD)
            ref[:, z * 2 * HD : (z + 1) * 2 * HD] = f_ref[:, pl.ds(start, 2 * HD)]


def join_kernel(*refs):
    for index, ref in enumerate(refs[:-1]):
        refs[-1][index] = ref[...]


def gate_kernel():
    pass


def near_kernel(place_ref, *refs):
    v_refs, f_refs, (part_ref, other_ref, v_ref, f_ref) = refs[:4], refs[4:8], refs[8:]
    y, z_lo = place_ref[4], place_ref[2]
    tok = f_refs[0].shape[0]
    for step, ref in enumerate(v_refs):
        cols = pl.ds(pl.multiple_of(lax.rem(y + step, 4) * tok, tok), tok)
        v_ref[:, cols] = ref[:, pl.ds(pl.multiple_of(z_lo * tok, tok), tok)]
        other_ref[:, cols] = ref[:, pl.ds(pl.multiple_of((1 - z_lo) * tok, tok), tok)]
    for step, ref in enumerate(f_refs):
        block = lax.rem(y + 4 - step, 4)
        f_ref[pl.ds(pl.multiple_of(block * tok, tok), tok), :] = ref[...]
    for z in range(4):
        cols = slice(z * 2 * HD, (z + 1) * 2 * HD)
        part_ref[:, cols] = dot(v_ref[...], f_ref[:, cols], NN)


def far_kernel(place_ref, part_ref, v_ref, *refs):
    own_ref, rest_ref, keep_ref, send_ref, f_ref = refs
    y, core = place_ref[4], place_ref[1]
    tok = own_ref.shape[0]
    for step, ref in enumerate((own_ref, *(rest_ref.at[i] for i in range(3)))):
        block = lax.rem(y + 4 - step, 4)
        f_ref[pl.ds(pl.multiple_of(block * tok, tok), tok), :] = ref[...]
    for z in range(4):
        cols = slice(z * 2 * HD, (z + 1) * 2 * HD)
        total = part_ref[:, cols] + dot(v_ref[...], f_ref[:, cols], NN)
        mine = jnp.where(core == 0, total[:, :HD], total[:, HD:])
        other = jnp.where(core == 0, total[:, HD:], total[:, :HD]).astype(BF16)
        for e in range(4):
            keep_ref[e, z] = mine[e * HD : (e + 1) * HD]
            send_ref[e, z] = other[e * HD : (e + 1) * HD]


def add_kernel(place_ref, keep_ref, got_ref, *out_refs):
    for step, ref in enumerate(out_refs):
        e = lax.rem(place_ref[0] + step, 4)
        ref[...] = (keep_ref[e] + got_ref[e].astype(F32)).astype(BF16)


def sum_kernel(place_ref, *refs):
    got_refs, (keep_ref, send_ref) = refs[:4], refs[4:]
    z_hi = place_ref[3]
    beside = z_hi + 1 - 2 * lax.rem(z_hi, 2)

    def summed(block):
        total = got_refs[0][block].astype(F32)
        for ref in got_refs[1:]:
            total += ref[block].astype(F32)
        return total

    for index in range(2):
        send_ref[index] = summed(beside + index * (3 - 2 * beside)).astype(BF16)
        keep_ref[index] = summed(z_hi + index * (3 - 2 * z_hi))


def pair_kernel(keep_ref, got_ref, own_ref, send_ref):
    own_ref[...] = keep_ref[0] + got_ref[0].astype(F32)
    send_ref[...] = keep_ref[1] + got_ref[1].astype(F32)


def last_kernel(own_ref, got_ref, out_ref):
    out_ref[...] = (own_ref[...] + got_ref[...]).T


def pack_rows_kernel(place_ref, own_ref, a_ref, b_ref, c_ref, out_ref):
    other = 1 - place_ref[2]
    out_ref[0] = own_ref[0, other]
    for step, ref in enumerate((a_ref, b_ref, c_ref)):
        out_ref[step + 1] = ref[other]


def assemble_kernel(place_ref, own_ref, a_ref, b_ref, c_ref, far_ref, q_ref, k_ref, done_ref):
    done_ref[...] = jnp.zeros_like(done_ref)
    x, z_lo = place_ref[0], place_ref[2]

    def put(rows, z, step):
        src = z * 4 + lax.rem(x + 4 - step, 4)
        q_ref[:, pl.ds(pl.multiple_of(src * 2 * HD, 2 * HD), 2 * HD)] = rows[:, : 2 * HD]
        k_ref[:, pl.ds(pl.multiple_of(src * HD, HD), HD)] = rows[:, 2 * HD :]

    put(own_ref[0, z_lo], z_lo, 0)
    for step, ref in enumerate((a_ref, b_ref, c_ref)):
        put(ref[z_lo], z_lo, step + 1)
    for step in range(4):
        put(far_ref[step], 1 - z_lo, step)


def call(
    kernel, shapes, *args, place=None, after=(), behind=(), anywhere=False, flops=0,
    nbytes=1 << 20, scratch=(),
):
    space = pltpu.MemorySpace.HBM if anywhere else pltpu.VMEM
    specs = [pl.BlockSpec(memory_space=space)] * len(args)
    shapes = list(shapes) if isinstance(shapes, (list, tuple)) else [shapes]
    out_specs = [pl.BlockSpec(memory_space=pltpu.VMEM)] * len(shapes)
    if place is not None:
        args = (place,) + args
        specs = [pl.BlockSpec(memory_space=pltpu.SMEM)] + specs
    n_in, n_out, n_after, n_behind = len(args), len(shapes), len(after), len(behind)
    args += tuple(after) + tuple(behind)
    specs += [pl.BlockSpec(memory_space=pl.ANY)] * (n_after + n_behind)
    shapes += [jax.ShapeDtypeStruct(x.shape, x.dtype) for x in behind]
    out_specs += [pl.BlockSpec(memory_space=pl.ANY)] * n_behind
    first_out = n_in + n_after + n_behind

    def body(*refs):
        outs = refs[first_out : first_out + n_out]
        kernel(*refs[:n_in], *outs, *refs[first_out + n_out + n_behind :])

    outs = pl.pallas_call(
        body,
        out_shape=shapes,
        in_specs=specs,
        out_specs=out_specs,
        scratch_shapes=list(scratch),
        input_output_aliases={n_in + n_after + i: n_out + i for i in range(n_behind)},
        compiler_params=params(),
        cost_estimate=pl.CostEstimate(flops=flops, bytes_accessed=nbytes, transcendentals=0),
    )(*args)
    return outs if len(outs) > 1 else outs[0]


def shape_of(*dims, dtype=BF16):
    return jax.ShapeDtypeStruct(dims, dtype)


def shift(array, axis, size, by):
    return lax.ppermute(array, axis, [(i, (i + by) % size) for i in range(size)])


def on_device(queries, key_heads, value_heads, grad_out, features):
    q, k, v = queries[0], key_heads[0], value_heads[0]
    length = q.shape[0]
    seq = ("z_lo", "x")
    place = jnp.stack([lax.axis_index(a) for a in ("x", "core", "z_lo", "z_hi", "y")]).astype(jnp.int32)
    tok = grad_out.shape[1]
    width = features.shape[2] // 4

    cot_parts = call(pack_cot_kernel, shape_of(8, tok, 2 * HD), grad_out[0])
    cot = lax.all_to_all(cot_parts, seq, 0, 0).reshape(length, 2 * HD)

    parts = call(
        pack_features_kernel,
        [shape_of(tok, width)] * 4,
        features[0],
        place=place,
        after=[cot_parts],
        nbytes=2 << 20,
    )
    near = [shift(parts[step], "y", 4, step) for step in range(1, 4)]
    far = shift(parts[0], "z_lo", 2, 1)

    probs = probs_of(q, k)
    pieces = call(
        value_kernel,
        [shape_of(HD, 2 * tok)] * 4,
        probs, cot,
        place=place,
        flops=1 << 29,
        nbytes=5 << 20,
        scratch=[pltpu.VMEM((HD, length), BF16)],
    )
    dv = pieces[0]
    pieces = [dv] + [shift(pieces[step], "x", 4, step) for step in range(1, 4)]
    columns = call(columns_kernel, shape_of(4 * HD, 2 * tok), *pieces, place=place)
    rest = call(join_kernel, shape_of(3, tok, width), *near, after=[dv, far], nbytes=2 << 20)
    near = [parts[0], *near]
    far = [far, shift(rest, "z_lo", 2, 1)]

    values = [columns] + [shift(columns, "y", 4, -step) for step in range(1, 4)]

    moved = grads_of(place, probs, q, k, v, cot, dv)
    half = length // 2
    part, other = call(
        near_kernel,
        [shape_of(4 * HD, width, dtype=F32), shape_of(4 * HD, half)],
        *values, *near,
        place=place,
        after=[moved],
        flops=0,
        nbytes=0,
        scratch=[pltpu.VMEM((4 * HD, half), BF16), pltpu.VMEM((half, width), BF16)],
    )
    keep, send = call(
        far_kernel,
        [shape_of(4, 4, HD, HD, dtype=F32), shape_of(4, 4, HD, HD)],
        part, other, *far,
        place=place,
        flops=LONG,
        nbytes=5 << 20,
        scratch=[pltpu.VMEM((half, width), BF16)],
    )
    got_x = [shift(moved[step], "x", 4, step) for step in range(1, 4)]
    send = call(gate_kernel, [], after=got_x, behind=[send])
    both = call(
        add_kernel, [shape_of(4, HD, HD)] * 4, keep, shift(send, "core", 2, 1), place=place
    )
    over_x = [both[0]] + [shift(both[step], "x", 4, step) for step in range(1, 4)]
    keep, send = call(
        sum_kernel,
        [shape_of(2, HD, HD, dtype=F32), shape_of(2, HD, HD)],
        *over_x,
        place=place,
        flops=LONG,
    )
    got = lax.ppermute(send, "z_hi", [(z, z ^ 1) for z in range(4)])
    own, send = call(pair_kernel, [shape_of(HD, HD, dtype=F32)] * 2, keep, got)
    got = lax.ppermute(send, "z_hi", [(z, 3 - z) for z in range(4)])
    packed = call(
        pack_rows_kernel, shape_of(4, tok, 3 * HD), moved, *got_x, place=place, after=[both[0]]
    )
    got_z = shift(packed, "z_lo", 2, 1)
    query_grad, key_grad, done = call(
        assemble_kernel,
        (shape_of(tok, 16 * HD), shape_of(tok, 8 * HD), shape_of(8, HD, dtype=F32)),
        moved, *got_x, got_z,
        place=place,
        after=[own],
    )
    weight_grad = call(last_kernel, shape_of(HD, HD, dtype=F32), own, got, after=[done])
    return query_grad[None], key_grad[None], weight_grad


def solution(mesh):
    fine = Mesh(mesh.devices.reshape(2, 4, 4, 4, 2), ("z_lo", "x", "z_hi", "y", "core"))
    seq, dp = ("z_lo", "x"), ("z_hi", "y", "core")
    return jax.shard_map(
        on_device,
        mesh=fine,
        in_specs=(P(dp, None, seq), P(dp, None, seq), P(dp, None, seq), P(dp, seq, None), P(dp, seq, None)),
        out_specs=(P(dp, seq, None), P(dp, seq, None), P(dp, seq)),
        check_vma=False,
    )
```
